512 devices in a mesh: lon: 64 (over z, x_hi, core), lat: 8 (over x_lo, y).
Axes of the slice: x: 4 (x_hi: 2, x_lo: 2; x = x_hi * 2 + x_lo), y: 4, z: 16, core: 2. Of those that a mesh axis runs over, the one named last changes fastest.
Arguments:
- patches: bfloat16 [2, 48, 1536, 512], P(None, 'lat', 'lon'), may hold values from -6 to 6
- regions: int32 [2, 48, 1536], P(None, 'lat', 'lon'), may hold values from 0 to 2, as said below
- w_qkv: bfloat16 [512, 1536], replicated, may hold values from -0.25 to 0.25
- w_out: bfloat16 [512, 512], replicated, may hold values from -1 to 1
Outputs:
- updated: bfloat16 [2, 48, 1536, 512], P(None, 'lat', 'lon')
The draws below stay inside these ranges and needn't reach their ends.
Inputs may be any that keep to these rules, and one draw needn't show every extreme that they name: `regions`: constant over aligned tiles of 3 latitude by 6 longitude patches, and the same at every level.
All inputs are finite; a program needn't handle non-finite values.
Results may differ from the reference program's by a relative error of at most 0.0065.
Values may be sent and summed in bfloat16 or wider, within the bound.
A program may use at most 64 MiB of HBM per device.

```python
import math
import jax
import jax.numpy as jnp
from jax import lax

D = 512
HEADS = 16
LV = 2
WIN_H = 6
WIN_W = 12
SHIFT_H = 3
SHIFT_W = 6
NLAT = 48
NLON = 1536


def draw_regions(key, part):
    key = jax.random.fold_in(key, 7)
    tiles = jax.random.randint(key, (NLAT // SHIFT_H, NLON // SHIFT_W), 0, 3, dtype=jnp.int32)
    field = jnp.repeat(jnp.repeat(tiles, SHIFT_H, axis=0), SHIFT_W, axis=1)
    return jnp.broadcast_to(field[None], (LV, NLAT, NLON)).astype(jnp.int32)


def steps_of(key, dims, shards, smallest, high):
    factor_of = 1.0
    for position, shards_of in shards:
        heights = jax.random.uniform(jax.random.fold_in(jax.random.fold_in(key, 6), position), (shards_of,), jnp.float32, smallest / len(shards), high / len(shards))
        factor_of = factor_of * jnp.repeat(jnp.exp(heights), dims[position] // shards_of).reshape((-1,) + (1,) * (len(dims) - 1 - position))
    return factor_of


def bell_draw(stream_key, shape, scale, limit, cuts=(), kind=jnp.bfloat16):
    drawn = scale * jax.random.normal(stream_key, shape, jnp.float32)
    if cuts:
        drawn = drawn * steps_of(stream_key, shape, cuts, -0.22, 0.18)
    return jnp.clip(drawn, -limit, limit).astype(kind)


def setup_inputs(seed: int = 0) -> dict:
    arg_keys = jax.random.split(jax.random.key(seed), 5)
    return {
        "patches": bell_draw(arg_keys[0], (LV, NLAT, NLON, D), 1.0, 6.0, ((1, 8), (2, 64))),
        "regions": draw_regions(jax.random.fold_in(arg_keys[4], 71), 0),
        "w_qkv": bell_draw(arg_keys[2], (D, 3 * D), D ** -0.5, 0.25),
        "w_out": bell_draw(arg_keys[3], (D, D), (D // 16) ** -0.5, 1.0),
    }


def layer_norm(source):
    values = source.astype(jnp.float32)
    center = values - lax.optimization_barrier(jnp.mean(values, axis=-1, keepdims=True))
    spread = lax.optimization_barrier(jnp.mean(center * center, axis=-1, keepdims=True))
    return (center * lax.rsqrt(spread + 1e-05)).astype(jnp.bfloat16)

def to_windows(source):
    levels, row_count, col_count, feature_count = source.shape
    source = source.reshape(levels, row_count // WIN_H, WIN_H, col_count // WIN_W, WIN_W, feature_count)
    source = source.transpose(1, 3, 0, 2, 4, 5)
    return source.reshape(row_count // WIN_H, col_count // WIN_W, levels * WIN_H * WIN_W, feature_count)

def from_windows(source, levels, row_count, col_count):
    feature_count = source.shape[-1]
    source = source.reshape(row_count // WIN_H, col_count // WIN_W, levels, WIN_H, WIN_W, feature_count)
    source = source.transpose(2, 0, 3, 1, 4, 5)
    return source.reshape(levels, row_count, col_count, feature_count)

def attend(window_block, region_ids, polar_rows, w_qkv):
    levels, row_count, col_count, width = window_block.shape
    normed = layer_norm(window_block)
    projected = jnp.dot(normed.reshape(-1, width), w_qkv, preferred_element_type=jnp.float32).astype(jnp.bfloat16)
    projected = to_windows(projected.reshape(levels, row_count, col_count, 3 * width))
    labels = to_windows(region_ids[..., None])[..., 0]
    pole_class = to_windows(jnp.broadcast_to(polar_rows[None, :, None, None], (levels, row_count, col_count, 1)))[..., 0]
    head_depth = width // HEADS

    def one_band(pieces):
        band_qkv, band_labels, band_poles = pieces
        window_count, window_size = (band_qkv.shape[0], band_qkv.shape[1])
        queries = band_qkv[..., :width].reshape(window_count, window_size, HEADS, head_depth).astype(jnp.float32)
        key_vecs = band_qkv[..., width:2 * width].reshape(window_count, window_size, HEADS, head_depth).astype(jnp.float32)
        values = band_qkv[..., 2 * width:].reshape(window_count, window_size, HEADS, head_depth).astype(jnp.float32)
        visible = (band_labels[:, :, None] == band_labels[:, None, :]) & (band_poles[:, :, None] == band_poles[:, None, :])
        scores = jnp.einsum('wqhd,wkhd->whqk', queries, key_vecs) * (1.0 / math.sqrt(head_depth))
        weights = jnp.where(visible[:, None], jnp.exp(scores), jnp.float32(0.0))
        weights = (weights / lax.optimization_barrier(jnp.sum(weights, axis=-1, keepdims=True))).astype(jnp.bfloat16)
        result = jnp.einsum('whqk,wkhd->wqhd', weights.astype(jnp.float32), values)
        return result.astype(jnp.bfloat16).reshape(window_count, window_size, width)
    attended = lax.map(one_band, (projected, labels, pole_class))
    return from_windows(attended, levels, row_count, col_count)

def reference(patches, regions, w_qkv, w_out):
    levels, height, lon_cells, width = patches.shape
    rolled = jnp.roll(patches, (-SHIFT_H, -SHIFT_W), axis=(1, 2))
    rolled_ids = jnp.roll(regions, (-SHIFT_H, -SHIFT_W), axis=(1, 2))

    def one_row(band_index):
        first_row = band_index * WIN_H
        window_block = lax.dynamic_slice_in_dim(rolled, first_row, WIN_H, 1)
        row_ids = lax.dynamic_slice_in_dim(rolled_ids, first_row, WIN_H, 1)
        global_rows = first_row + jnp.arange(WIN_H, dtype=jnp.int32)
        polar_rows = (global_rows >= height - SHIFT_H).astype(jnp.int32)
        attended = attend(window_block, row_ids, polar_rows, w_qkv)
        output = jnp.dot(attended.reshape(-1, width), w_out, preferred_element_type=jnp.float32)
        return (window_block.astype(jnp.float32) + output.reshape(window_block.shape)).astype(jnp.bfloat16)
    result = lax.map(one_row, jnp.arange(height // WIN_H, dtype=jnp.int32))
    result = result.transpose(1, 0, 2, 3, 4).reshape(levels, height, lon_cells, width)
    return jnp.roll(result, (SHIFT_H, SHIFT_W), axis=(1, 2))
```

```python
import math

import jax
import jax.numpy as jnp
from jax import lax
from jax.experimental import pallas as pl
from jax.experimental.pallas import tpu as pltpu
from jax.sharding import PartitionSpec as P

HEADS = 16
WIN_H = 6
WIN_W = 12
SHIFT_H = 3
SHIFT_W = 6
LEVELS = 2
TILE = 8
MESH = pl.DeviceIdType.MESH
F32 = jnp.float32
BF16 = jnp.bfloat16

EAST, EAST_N, EAST_S = 0, 1, 2
WEST, WEST_N, WEST_S = 3, 4, 5
NORTH, SOUTH = 6, 7
WAYS = ((1, 0), (1, -1), (1, 1), (-1, 0), (-1, -1), (-1, 1), (0, -1), (0, 1))
EASTWARD = (EAST, EAST_N, EAST_S)
WESTWARD = (WEST, WEST_N, WEST_S)


def layer_norm(values):
    center = values - jnp.mean(values, axis=-1, keepdims=True)
    spread = jnp.mean(center * center, axis=-1, keepdims=True)
    return (center * lax.rsqrt(spread + 1e-05)).astype(BF16)


def attend(queries, key_vecs, values, bias):
    query_count, width = queries.shape
    key_count = key_vecs.shape[0]
    head_depth = width // HEADS
    scale = math.log2(math.e) / math.sqrt(head_depth)
    per_group = 128 // head_depth
    lane = lax.broadcasted_iota(jnp.int32, (1, 128), 1) // head_depth
    only = [(lane == head).astype(F32).astype(BF16) for head in range(per_group)]
    ones = jnp.ones((key_count, 128), BF16)
    sums, totals = [], []
    for group in range(width // 128):
        part = slice(group * 128, (group + 1) * 128)
        spread = jnp.concatenate([queries[:, part] * mask for mask in only], axis=0)
        scores = lax.dot_general(
            spread, key_vecs[:, part], (((1,), (1,)), ((), ())), preferred_element_type=F32
        )
        scores = scores.reshape(per_group, query_count, key_count)
        weights = jnp.exp2(scores * scale + bias[None]).astype(BF16)
        result = jnp.dot(
            weights.reshape(per_group * query_count, key_count),
            jnp.concatenate([values[:, part], ones], axis=1),
            preferred_element_type=F32,
        ).reshape(per_group, query_count, 256)
        chosen = result[per_group - 1]
        lanes = lax.broadcasted_iota(jnp.int32, (query_count, 256), 1) % 128 // head_depth
        for head in range(per_group - 1):
            chosen = jnp.where(lanes == head, result[head], chosen)
        sums.append(chosen[:, :128])
        totals.append(chosen[:, 128:])
    return jnp.concatenate(sums, axis=1), jnp.concatenate(totals, axis=1)


def bias_of(query_code, key_code):
    return jnp.where(query_code == key_code, F32(-8.0), F32(-1e30))


def row_code(ids, shape, dim, cols):
    col = lax.broadcasted_iota(jnp.int32, shape, dim) % cols
    code = jnp.broadcast_to(ids[0], shape)
    for block in range(1, 4):
        code = jnp.where(col >= block * SHIFT_W, ids[block] + 4 * ((block + 1) // 2), code)
    return code


def kernel(
    n_lon, n_lat,
    x_hbm, ids_hbm, w_qkv_hbm, w_out_hbm,
    out_ref,
    x, w_qkv, w_out, ids, north, south, east, west, halo_ids, queries, sums, totals,
    load_sem, send_sem, recv_sem, ready,
):
    lon, lat = lax.axis_index("lon"), lax.axis_index("lat")
    first, last, before = lon == 0, lon == n_lon - 1, lon == n_lon - 2
    has_north, has_south = lat > 0, lat < n_lat - 1
    more_north, more_south = jnp.where(has_north, 1, 0), jnp.where(has_south, 1, 0)
    three = 1 + more_north + more_south
    width = x.shape[-1]
    half_tokens = LEVELS * SHIFT_H * 3 * TILE

    def device(way):
        dlon, dlat = WAYS[way]
        return {"lon": lax.rem(lon + dlon + n_lon, n_lon), "lat": lax.rem(lat + dlat + n_lat, n_lat)}

    def exists(way):
        dlat = WAYS[way][1]
        return has_north if dlat < 0 else has_south if dlat > 0 else None

    def comes(way):
        dlat = WAYS[way][1]
        return has_south if dlat < 0 else has_north if dlat > 0 else None

    def when(condition, do):
        def run():
            do()

        if condition is None:
            run()
        else:
            pl.when(condition)(run)

    def signal_all(semaphore, ways):
        for way in ways:
            when(
                exists(way),
                lambda way=way: pl.semaphore_signal(
                    semaphore, inc=1, device_id=device(way), device_id_type=MESH
                ),
            )

    def rows_sent(way):
        return {0: pl.ds(0, 6), -1: pl.ds(0, 3), 1: pl.ds(3, 3)}[WAYS[way][1]]

    def copies(way):
        dlon, dlat = WAYS[way]
        rows = rows_sent(way)
        lands = {0: pl.ds(3, 6), -1: pl.ds(9, 3), 1: pl.ds(0, 3)}[dlat]
        if dlon == 0:
            pair = (x_hbm.at[:, rows], (south if dlat < 0 else north))
        elif dlon > 0:
            pair = (x_hbm.at[:, rows, 2], west.at[:, lands])
        else:
            pair = (x_hbm.at[:, rows, 0], east.at[:, lands])
        pairs = (pair, (ids_hbm, halo_ids.at[way]))
        return [
            pltpu.make_async_remote_copy(
                src_ref=source,
                dst_ref=target,
                send_sem=send_sem.at[way, part],
                recv_sem=recv_sem.at[way, part],
                device_id=device(way),
                device_id_type=MESH,
            )
            for part, (source, target) in enumerate(pairs)
        ]

    def send(ways):
        for way in ways:
            when(exists(way), lambda way=way: [copy.start() for copy in copies(way)])

    def wait_recv(ways):
        for way in ways:
            when(comes(way), lambda way=way: [copy.wait_recv() for copy in copies(way)])

    def wait_send(ways):
        for way in ways:
            when(exists(way), lambda way=way: [copy.wait_send() for copy in copies(way)])

    barrier = pltpu.get_barrier_semaphore()
    ready_east, ready_west, ready_south = ready.at[0], ready.at[1], ready.at[2]
    inner = jnp.logical_not(jnp.logical_or(first, last))
    to_east = jnp.logical_or(before, last)
    pl.when(jnp.logical_not(to_east))(lambda: signal_all(barrier, EASTWARD))
    pl.when(jnp.logical_not(inner))(lambda: signal_all(barrier, WESTWARD))
    pl.when(jnp.logical_not(last))(lambda: signal_all(barrier, (SOUTH,)))

    loads = [
        pltpu.make_async_copy(source, target, load_sem.at[index])
        for index, (source, target) in enumerate(
            ((x_hbm, x), (ids_hbm, ids), (w_qkv_hbm, w_qkv), (w_out_hbm, w_out))
        )
    ]
    for load in loads:
        load.start()

    greeted = (
        jnp.where(inner, three, 0)
        + jnp.where(to_east, three, 0)
        + jnp.where(jnp.logical_not(last), more_north, 0)
    )

    @pl.when(greeted > 0)
    def _():
        pl.semaphore_wait(barrier, greeted)

    @pl.when(to_east)
    def _():
        send((EAST_N, EAST_S, EAST))
        signal_all(ready_west, EASTWARD)

    @pl.when(inner)
    def _():
        signal_all(ready_east, WESTWARD)

    @pl.when(jnp.logical_not(last))
    def _():
        signal_all(ready_south, (NORTH,))

    @pl.when(inner)
    def _():
        send(WESTWARD)

    @pl.when(jnp.logical_not(last))
    def _():
        send((NORTH,))

    @pl.when(jnp.logical_not(has_north))
    def _():
        east[:, 0:3] = jnp.zeros((LEVELS, 3, TILE, width), BF16)
        west[:, 0:3] = jnp.zeros((LEVELS, 3, TILE, width), BF16)
        for way in (EAST_S, WEST_S):
            halo_ids[way] = jnp.zeros(halo_ids.shape[1:], jnp.int32)

    @pl.when(jnp.logical_not(has_south))
    def _():
        east[:, 9:12] = jnp.zeros((LEVELS, 3, TILE, width), BF16)
        west[:, 9:12] = jnp.zeros((LEVELS, 3, TILE, width), BF16)
        for way in (EAST_N, WEST_N):
            halo_ids[way] = jnp.zeros(halo_ids.shape[1:], jnp.int32)

    def class_of(ref, row, block):
        return ref[row, 0:1, block * SHIFT_W : block * SHIFT_W + 1]

    def classes(ref, row):
        return [class_of(ref, row, block) for block in range(4)]

    def query_code(half):
        return row_code(classes(ids, 3 * half), (half_tokens, 1), 0, 24)

    def halo_projection(source):
        normed = layer_norm(source.astype(F32).reshape(-1, width))
        both = jnp.dot(normed, w_qkv[:, width:], preferred_element_type=F32).astype(BF16)
        return both[:, :width], both[:, width:]

    for load in loads[:3]:
        load.wait()
    block = (LEVELS, 3, 3, TILE, width)
    for half in range(2):
        rows = slice(3 * half, 3 * half + 3)
        normed = layer_norm(x[:, rows].astype(F32).reshape(half_tokens, width))
        projected = jnp.dot(normed, w_qkv[...], preferred_element_type=F32)
        queries[:, rows] = projected[:, :width].reshape(block)
        projected = projected.astype(BF16)
        key_code = row_code(classes(ids, 3 * half), (1, half_tokens), 1, 24)
        some, total = attend(
            projected[:, :width],
            projected[:, width : 2 * width],
            projected[:, 2 * width :],
            bias_of(query_code(half), key_code),
        )
        sums[:, rows] = some.reshape(block)
        totals[:, rows] = total.reshape(block)

    @pl.when(jnp.logical_not(to_east))
    def _():
        pl.semaphore_wait(ready_east, three)
        send(EASTWARD)

    @pl.when(jnp.logical_and(jnp.logical_not(last), has_south))
    def _():
        pl.semaphore_wait(ready_south, 1)
        send((SOUTH,))

    @pl.when(last)
    def _():
        pl.semaphore_wait(ready_west, three)
        send((NORTH, SOUTH) + WESTWARD)

    def row_halo(half, source, way):
        rows = slice(3 * half, 3 * half + 3)
        key_vecs, values = halo_projection(source[...])
        key_code = row_code(classes(halo_ids.at[way], 3 - 3 * half), (1, half_tokens), 1, 24)
        some, total = attend(
            queries[:, rows].reshape(half_tokens, width).astype(BF16),
            key_vecs,
            values,
            bias_of(query_code(half), key_code),
        )
        sums[:, rows] += some.reshape(block)
        totals[:, rows] += total.reshape(block)

    @pl.when(has_north)
    def _():
        wait_recv((SOUTH,))
        row_halo(0, north, SOUTH)

    @pl.when(has_south)
    def _():
        wait_recv((NORTH,))
        row_halo(1, south, NORTH)

    def side_halo(tile, source, ways, query_block, key_block, query_cols, key_cols):
        straight, from_south, from_north = ways
        key_vecs, values = halo_projection(source[...])
        token = lax.broadcasted_iota(jnp.int32, (LEVELS * 6 * TILE, 1), 0)
        col, row = token % TILE, token // TILE % 6
        mine = jnp.where(
            row >= 3, class_of(ids, 3, query_block) + 4, class_of(ids, 0, query_block)
        )
        mine = jnp.where((col >= query_cols[0]) & (col < query_cols[1]), mine, -2)
        token = lax.broadcasted_iota(jnp.int32, (1, LEVELS * 12 * TILE), 1)
        col, row = token % TILE, token // TILE % 12
        theirs = jnp.where(
            row >= 9,
            class_of(halo_ids.at[from_south], 0, key_block) + 4,
            jnp.where(
                row >= 6,
                class_of(halo_ids.at[straight], 3, key_block) + 4,
                jnp.where(
                    row >= 3,
                    class_of(halo_ids.at[straight], 0, key_block),
                    class_of(halo_ids.at[from_north], 3, key_block),
                ),
            ),
        )
        seen = (col >= key_cols[0]) & (col < key_cols[1])
        seen = seen & ((row >= 3 * (1 - more_north)) & (row < 9 + 3 * more_south))
        theirs = jnp.where(seen, theirs, -1)
        some, total = attend(
            queries[:, :, tile].reshape(-1, width).astype(BF16), key_vecs, values, bias_of(mine, theirs)
        )
        side = (LEVELS, 6, TILE, width)
        return sums[:, :, tile] + some.reshape(side), totals[:, :, tile] + total.reshape(side)

    def finish(patches, some, total):
        attended = (some / total).astype(BF16).reshape(-1, width)
        output = jnp.dot(attended, w_out[...], preferred_element_type=F32)
        return (patches.astype(F32) + output.reshape(patches.shape)).astype(BF16)

    wait_recv(WESTWARD)
    some, total = side_halo(2, east, WESTWARD, 3, 0, (2, 8), (0, 6))
    loads[3].wait()
    out_ref[:, :, 2] = finish(x[:, :, 2], some, total)
    out_ref[:, :, 1] = finish(x[:, :, 1], sums[:, :, 1], totals[:, :, 1])

    @pl.when(first)
    def _():
        pl.semaphore_wait(ready_west, three)
        send(WESTWARD)

    wait_recv(EASTWARD)
    some, total = side_halo(0, west, EASTWARD, 0, 3, (0, 6), (2, 8))
    out_ref[:, :, 0] = finish(x[:, :, 0], some, total)

    wait_send(range(len(WAYS)))


def shards(n_lon, n_lat, patches, regions, w_qkv, w_out):
    levels, row_count, col_count, width = patches.shape
    tiles = (levels, row_count, col_count // TILE, TILE, width)
    half = (levels, SHIFT_H, col_count // TILE, TILE, width)
    side = (levels, row_count + 2 * SHIFT_H, TILE, width)
    id_shape = (row_count, levels, col_count)
    hbm = pl.BlockSpec(memory_space=pltpu.HBM)
    updated = pl.pallas_call(
        lambda *refs: kernel(n_lon, n_lat, *refs),
        out_shape=jax.ShapeDtypeStruct(tiles, BF16),
        in_specs=[hbm] * 4,
        out_specs=pl.BlockSpec(memory_space=pltpu.VMEM),
        scratch_shapes=[
            pltpu.VMEM(tiles, BF16),
            pltpu.VMEM(w_qkv.shape, BF16),
            pltpu.VMEM(w_out.shape, BF16),
            pltpu.VMEM(id_shape, jnp.int32),
            pltpu.VMEM(half, BF16),
            pltpu.VMEM(half, BF16),
            pltpu.VMEM(side, BF16),
            pltpu.VMEM(side, BF16),
            pltpu.VMEM((len(WAYS),) + id_shape, jnp.int32),
            pltpu.VMEM(tiles, F32),
            pltpu.VMEM(tiles, F32),
            pltpu.VMEM(tiles, F32),
            pltpu.SemaphoreType.DMA((4,)),
            pltpu.SemaphoreType.DMA((len(WAYS), 2)),
            pltpu.SemaphoreType.DMA((len(WAYS), 2)),
            pltpu.SemaphoreType.REGULAR((3,)),
        ],
        compiler_params=pltpu.CompilerParams(
            collective_id=0, has_side_effects=True, vmem_limit_bytes=60 * 2**20
        ),
    )(patches.reshape(tiles), regions.transpose(1, 0, 2), w_qkv, w_out)
    return updated.reshape(patches.shape)


def solution(mesh):
    n_lon, n_lat = mesh.shape["lon"], mesh.shape["lat"]
    return jax.shard_map(
        lambda *arrays: shards(n_lon, n_lat, *arrays),
        mesh=mesh,
        in_specs=(P(None, "lat", "lon", None), P(None, "lat", "lon"), P(), P()),
        out_specs=P(None, "lat", "lon", None),
        check_vma=False,
    )
```

```python
import math

import jax
import jax.numpy as jnp
from jax import lax
from jax.experimental import pallas as pl
from jax.experimental.pallas import tpu as pltpu
from jax.sharding import PartitionSpec as P

HEADS = 16
WIN_H = 6
WIN_W = 12
SHIFT_H = 3
SHIFT_W = 6
LEVELS = 2
TILE = 8
MESH = pl.DeviceIdType.MESH
F32 = jnp.float32
BF16 = jnp.bfloat16

EAST, EAST_N, EAST_S = 0, 1, 2
WEST, WEST_N, WEST_S = 3, 4, 5
NORTH, SOUTH = 6, 7
WAYS = ((1, 0), (1, -1), (1, 1), (-1, 0), (-1, -1), (-1, 1), (0, -1), (0, 1))
EASTWARD = (EAST, EAST_N, EAST_S)
WESTWARD = (WEST, WEST_N, WEST_S)


def layer_norm(values):
    center = values - jnp.mean(values, axis=-1, keepdims=True)
    spread = jnp.mean(center * center, axis=-1, keepdims=True)
    return (center * lax.rsqrt(spread + 1e-05)).astype(BF16)


def attend(queries, key_vecs, values, bias):
    query_count, width = queries.shape
    key_count = key_vecs.shape[0]
    head_depth = width // HEADS
    scale = math.log2(math.e) / math.sqrt(head_depth)
    per_group = 128 // head_depth
    lane = lax.broadcasted_iota(jnp.int32, (1, 128), 1) // head_depth
    only = [(lane == head).astype(F32).astype(BF16) for head in range(per_group)]
    ones = jnp.ones((key_count, 128), BF16)
    sums, totals = [], []
    for group in range(width // 128):
        part = slice(group * 128, (group + 1) * 128)
        spread = jnp.concatenate([queries[:, part] * mask for mask in only], axis=0)
        scores = lax.dot_general(
            spread, key_vecs[:, part], (((1,), (1,)), ((), ())), preferred_element_type=F32
        )
        scores = scores.reshape(per_group, query_count, key_count)
        weights = jnp.exp2(scores * scale + bias[None]).astype(BF16)
        result = jnp.dot(
            weights.reshape(per_group * query_count, key_count),
            jnp.concatenate([values[:, part], ones], axis=1),
            preferred_element_type=F32,
        ).reshape(per_group, query_count, 256)
        chosen = result[per_group - 1]
        lanes = lax.broadcasted_iota(jnp.int32, (query_count, 256), 1) % 128 // head_depth
        for head in range(per_group - 1):
            chosen = jnp.where(lanes == head, result[head], chosen)
        sums.append(chosen[:, :128])
        totals.append(chosen[:, 128:])
    return jnp.concatenate(sums, axis=1), jnp.concatenate(totals, axis=1)


def bias_of(query_code, key_code):
    return jnp.where(query_code == key_code, F32(-8.0), F32(-1e30))


def row_code(ids, shape, dim, cols):
    col = lax.broadcasted_iota(jnp.int32, shape, dim) % cols
    code = jnp.broadcast_to(ids[0], shape)
    for block in range(1, 4):
        code = jnp.where(col >= block * SHIFT_W, ids[block] + 4 * ((block + 1) // 2), code)
    return code


def kernel(
    n_lon, n_lat,
    x_hbm, ids_hbm, w_qkv_hbm, w_out_hbm,
    out_ref,
    x, w_qkv, w_out, ids, beside, east, west, halo_ids, queries, sums, totals,
    load_sem, send_sem, recv_sem, ready,
):
    lon, lat = lax.axis_index("lon"), lax.axis_index("lat")
    first, last, before = lon == 0, lon == n_lon - 1, lon == n_lon - 2
    even = lax.rem(lon, 2) == 0
    odd = jnp.logical_not(even)
    crossed_west = jnp.logical_and(even, jnp.logical_not(first))
    crossed_east = jnp.logical_and(odd, jnp.logical_not(last))
    north, south = beside.at[0], beside.at[1]

    def east_first(lon):
        late_corner = jnp.logical_and(lon == 1, lat == 0)
        falling = jnp.logical_and(lax.rem(lon, 4) == 3, lon >= n_lon // 2)
        return (lon >= n_lon - 2) | (lon < 0) | late_corner | falling

    def south_first(lat):
        late_corner = jnp.logical_and(lat == 0, lon < 2)
        return jnp.logical_or(lax.rem(lat, n_lat // 2) == n_lat // 2 - 1, late_corner)

    has_north, has_south = lat > 0, lat < n_lat - 1
    more_north, more_south = jnp.where(has_north, 1, 0), jnp.where(has_south, 1, 0)
    three = 1 + more_north + more_south
    width = x.shape[-1]
    half_tokens = LEVELS * SHIFT_H * 3 * TILE

    def device(dlon, dlat):
        return {"lon": lax.rem(lon + dlon + n_lon, n_lon), "lat": lax.rem(lat + dlat + n_lat, n_lat)}

    def exists(way):
        dlat = WAYS[way][1]
        return has_north if dlat < 0 else has_south if dlat > 0 else None

    def comes(way):
        dlat = WAYS[way][1]
        return has_south if dlat < 0 else has_north if dlat > 0 else None

    def when(condition, do):
        def run():
            do()

        if condition is None:
            run()
        else:
            pl.when(condition)(run)

    def signal_all(semaphore, ways):
        for way in ways:
            when(
                exists(way),
                lambda way=way: pl.semaphore_signal(
                    semaphore, inc=1, device_id=device(*WAYS[way]), device_id_type=MESH
                ),
            )

    def message(way, sources, send_index, target):
        dlon, dlat = WAYS[way]
        lands = {0: pl.ds(3, 6), -1: pl.ds(9, 3), 1: pl.ds(0, 3)}[dlat]
        if dlon == 0:
            landing = south if dlat < 0 else north
        else:
            landing = (west if dlon > 0 else east).at[:, lands]
        return [
            pltpu.make_async_remote_copy(
                src_ref=source,
                dst_ref=place,
                send_sem=send_sem.at[send_index, part],
                recv_sem=recv_sem.at[way, part],
                device_id=device(*target),
                device_id_type=MESH,
            )
            for part, (source, place) in enumerate(zip(sources, (landing, halo_ids.at[way])))
        ]

    def direct(way):
        dlon, dlat = WAYS[way]
        rows = {0: pl.ds(0, 6), -1: pl.ds(0, 3), 1: pl.ds(3, 3)}[dlat]
        source = x_hbm.at[:, rows] if dlon == 0 else x_hbm.at[:, rows, 2 if dlon > 0 else 0]
        return message(way, (source, ids_hbm), way, WAYS[way])

    def send(ways):
        for way in ways:
            when(exists(way), lambda way=way: [copy.start() for copy in direct(way)])

    def wait_recv(ways):
        for way in ways:
            when(comes(way), lambda way=way: [copy.wait_recv() for copy in direct(way)])

    def wait_send(ways):
        for way in ways:
            when(exists(way), lambda way=way: [copy.wait_send() for copy in direct(way)])

    def chip_relays(way):
        source, edge = (north, has_north) if way == SOUTH else (south, has_south)
        to_east, to_west = (EAST_S, WEST_S) if way == SOUTH else (EAST_N, WEST_N)
        return [
            (
                jnp.logical_and(edge, even if dlon > 0 else odd),
                message(to, (source.at[:, :, 2 if dlon > 0 else 0], halo_ids.at[way]), to, (dlon, 0)),
            )
            for to, dlon in ((to_east, 1), (to_west, -1))
        ]

    def lat_relays(way):
        source = west if way == EAST else east
        parts = (
            (EAST_N if way == EAST else WEST_N, has_north, pl.ds(3, 3), -1),
            (EAST_S if way == EAST else WEST_S, has_south, pl.ds(6, 3), 1),
        )
        crossed = crossed_west if way == EAST else crossed_east
        return [
            (
                jnp.logical_and(edge, crossed),
                message(to, (source.at[:, rows], halo_ids.at[way]), len(WAYS) + to, (0, dlat)),
            )
            for to, edge, rows, dlat in parts
        ]

    def start(relays):
        for condition, copies in relays:
            when(condition, lambda copies=copies: [copy.start() for copy in copies])

    def finish_relays(relays):
        for condition, copies in relays:
            when(condition, lambda copies=copies: [copy.wait_send() for copy in copies])

    barrier = pltpu.get_barrier_semaphore()
    ready_east, ready_west, ready_north, ready_south = [ready.at[index] for index in range(4)]
    to_east = jnp.logical_or(before, last)
    not_last = jnp.logical_not(last)
    early_east, early_west = east_first(lon), jnp.logical_not(east_first(lon - 1))
    late_east, late_west = jnp.logical_not(early_east), jnp.logical_not(early_west)
    inner_south = jnp.logical_and(has_south, not_last)
    inner_north = jnp.logical_and(has_north, not_last)
    early_south = jnp.logical_and(inner_south, south_first(lat))
    late_south = jnp.logical_and(inner_south, jnp.logical_not(south_first(lat)))
    early_north = jnp.logical_and(inner_north, jnp.logical_not(south_first(lat - 1)))
    late_north = jnp.logical_and(inner_north, south_first(lat - 1))
    seam = jnp.logical_or(first, last)

    pl.when(late_east)(lambda: signal_all(barrier, (EAST,)))
    pl.when(jnp.logical_and(late_west, jnp.logical_not(seam)))(lambda: signal_all(barrier, (WEST,)))
    pl.when(seam)(lambda: signal_all(barrier, WESTWARD))
    pl.when(late_south)(lambda: signal_all(barrier, (SOUTH,)))
    pl.when(late_north)(lambda: signal_all(barrier, (NORTH,)))

    loads = [
        pltpu.make_async_copy(source, target, load_sem.at[index])
        for index, (source, target) in enumerate(
            ((x_hbm, x), (ids_hbm, ids), (w_qkv_hbm, w_qkv), (w_out_hbm, w_out))
        )
    ]

    def start_loads():
        for load in loads:
            load.start()

    pl.when(not_last)(start_loads)
    greeted = (
        jnp.where(early_west, 1, 0)
        + jnp.where(early_east, jnp.where(to_east, three, 1), 0)
        + jnp.where(jnp.logical_or(early_north, early_south), 1, 0)
        + jnp.where(jnp.logical_and(early_north, early_south), 1, 0)
    )

    @pl.when(greeted > 0)
    def _():
        pl.semaphore_wait(barrier, greeted)

    @pl.when(last)
    def _():
        send((EAST_N, EAST_S))

    @pl.when(early_east)
    def _():
        send((EAST,))

    pl.when(last)(lambda: signal_all(ready_west, EASTWARD))
    pl.when(jnp.logical_and(early_east, not_last))(lambda: signal_all(ready_west, (EAST,)))

    pl.when(last)(start_loads)

    @pl.when(early_west)
    def _():
        signal_all(ready_east, (WEST,))
        send((WEST,))

    @pl.when(early_north)
    def _():
        signal_all(ready_south, (NORTH,))
        send((NORTH,))

    @pl.when(early_south)
    def _():
        signal_all(ready_north, (SOUTH,))
        send((SOUTH,))

    @pl.when(jnp.logical_not(has_north))
    def _():
        east[:, 0:3] = jnp.zeros((LEVELS, 3, TILE, width), BF16)
        west[:, 0:3] = jnp.zeros((LEVELS, 3, TILE, width), BF16)
        for way in (EAST_S, WEST_S):
            halo_ids[way] = jnp.zeros(halo_ids.shape[1:], jnp.int32)

    @pl.when(jnp.logical_not(has_south))
    def _():
        east[:, 9:12] = jnp.zeros((LEVELS, 3, TILE, width), BF16)
        west[:, 9:12] = jnp.zeros((LEVELS, 3, TILE, width), BF16)
        for way in (EAST_N, WEST_N):
            halo_ids[way] = jnp.zeros(halo_ids.shape[1:], jnp.int32)

    def class_of(ref, row, block):
        return ref[row, 0:1, block * SHIFT_W : block * SHIFT_W + 1]

    def classes(ref, row):
        return [class_of(ref, row, block) for block in range(4)]

    def query_code(half):
        return row_code(classes(ids, 3 * half), (half_tokens, 1), 0, 24)

    def halo_projection(source):
        normed = layer_norm(source.astype(F32).reshape(-1, width))
        both = jnp.dot(normed, w_qkv[:, width:], preferred_element_type=F32).astype(BF16)
        return both[:, :width], both[:, width:]

    for load in loads[:3]:
        load.wait()
    block = (LEVELS, 3, 3, TILE, width)
    for half in range(2):
        rows = slice(3 * half, 3 * half + 3)
        normed = layer_norm(x[:, rows].astype(F32).reshape(half_tokens, width))
        projected = jnp.dot(normed, w_qkv[...], preferred_element_type=F32)
        queries[:, rows] = projected[:, :width].reshape(block)
        projected = projected.astype(BF16)
        key_code = row_code(classes(ids, 3 * half), (1, half_tokens), 1, 24)
        some, total = attend(
            projected[:, :width],
            projected[:, width : 2 * width],
            projected[:, 2 * width :],
            bias_of(query_code(half), key_code),
        )
        sums[:, rows] = some.reshape(block)
        totals[:, rows] = total.reshape(block)
        if half == 0:

            @pl.when(late_south)
            def _():
                pl.semaphore_wait(ready_south, 1)
                send((SOUTH,))

            @pl.when(late_north)
            def _():
                pl.semaphore_wait(ready_north, 1)
                send((NORTH,))

            @pl.when(last)
            def _():
                pl.semaphore_wait(ready_west, 1)
                send((NORTH, SOUTH, WEST))

    @pl.when(late_east)
    def _():
        pl.semaphore_wait(ready_east, 1)
        send((EAST,))

    @pl.when(jnp.logical_and(late_west, jnp.logical_not(seam)))
    def _():
        pl.semaphore_wait(ready_west, 1)
        send((WEST,))

    @pl.when(crossed_west)
    def _():
        wait_recv((EAST,))

    @pl.when(crossed_east)
    def _():
        wait_recv((WEST,))

    start(lat_relays(EAST) + lat_relays(WEST))

    def row_halo(half):
        rows = pl.ds(3 * half, 3)
        key_vecs, values = halo_projection(beside[half])
        their_ids = halo_ids.at[jnp.where(half == 0, SOUTH, NORTH)]
        key_code = row_code(classes(their_ids, 3 - 3 * half), (1, half_tokens), 1, 24)
        some, total = attend(
            queries[:, rows].reshape(half_tokens, width).astype(BF16),
            key_vecs,
            values,
            bias_of(query_code(half), key_code),
        )
        sums[:, rows] += some.reshape(block)
        totals[:, rows] += total.reshape(block)

    north_first = jnp.where(early_south, 1, 0)
    for step in range(2):
        half = 1 - north_first if step == 0 else north_first

        @pl.when(half == 0)
        def _():
            wait_recv((SOUTH,))
            start(chip_relays(SOUTH))

        @pl.when(half == 1)
        def _():
            wait_recv((NORTH,))
            start(chip_relays(NORTH))

        @pl.when(jnp.where(half == 0, more_north, more_south) == 1)
        def _():
            row_halo(half)

    def side_halo(tile, source, ways, query_block, key_block, query_cols, key_cols):
        straight, from_south, from_north = ways
        key_vecs, values = halo_projection(source[...])
        token = lax.broadcasted_iota(jnp.int32, (LEVELS * 6 * TILE, 1), 0)
        col, row = token % TILE, token // TILE % 6
        mine = jnp.where(
            row >= 3, class_of(ids, 3, query_block) + 4, class_of(ids, 0, query_block)
        )
        mine = jnp.where((col >= query_cols[0]) & (col < query_cols[1]), mine, -2)
        token = lax.broadcasted_iota(jnp.int32, (1, LEVELS * 12 * TILE), 1)
        col, row = token % TILE, token // TILE % 12
        theirs = jnp.where(
            row >= 9,
            class_of(halo_ids.at[from_south], 0, key_block) + 4,
            jnp.where(
                row >= 6,
                class_of(halo_ids.at[straight], 3, key_block) + 4,
                jnp.where(
                    row >= 3,
                    class_of(halo_ids.at[straight], 0, key_block),
                    class_of(halo_ids.at[from_north], 3, key_block),
                ),
            ),
        )
        seen = (col >= key_cols[0]) & (col < key_cols[1])
        seen = seen & ((row >= 3 * (1 - more_north)) & (row < 9 + 3 * more_south))
        theirs = jnp.where(seen, theirs, -1)
        some, total = attend(
            queries[:, :, tile].reshape(-1, width).astype(BF16), key_vecs, values, bias_of(mine, theirs)
        )
        side = (LEVELS, 6, TILE, width)
        return sums[:, :, tile] + some.reshape(side), totals[:, :, tile] + total.reshape(side)

    def finish(patches, some, total):
        attended = (some / total).astype(BF16).reshape(-1, width)
        output = jnp.dot(attended, w_out[...], preferred_element_type=F32)
        return (patches.astype(F32) + output.reshape(patches.shape)).astype(BF16)

    @pl.when(jnp.logical_not(crossed_east))
    def _():
        wait_recv((WEST,))

    wait_recv((WEST_N, WEST_S))
    some, total = side_halo(2, east, WESTWARD, 3, 0, (2, 8), (0, 6))
    loads[3].wait()
    out_ref[:, :, 2] = finish(x[:, :, 2], some, total)
    out_ref[:, :, 1] = finish(x[:, :, 1], sums[:, :, 1], totals[:, :, 1])

    @pl.when(first)
    def _():
        pl.semaphore_wait(ready_west, three)
        send(WESTWARD)

    @pl.when(jnp.logical_not(crossed_west))
    def _():
        wait_recv((EAST,))

    wait_recv((EAST_N, EAST_S))
    some, total = side_halo(0, west, EASTWARD, 0, 3, (0, 6), (2, 8))
    out_ref[:, :, 0] = finish(x[:, :, 0], some, total)

    wait_send((EAST, WEST, NORTH, SOUTH))

    @pl.when(last)
    def _():
        wait_send((EAST_N, EAST_S))

    @pl.when(first)
    def _():
        wait_send((WEST_N, WEST_S))

    for way in (NORTH, SOUTH):
        finish_relays(chip_relays(way))
    for way in (EAST, WEST):
        finish_relays(lat_relays(way))


def shards(n_lon, n_lat, patches, regions, w_qkv, w_out):
    levels, row_count, col_count, width = patches.shape
    tiles = (levels, row_count, col_count // TILE, TILE, width)
    half = (levels, SHIFT_H, col_count // TILE, TILE, width)
    side = (levels, row_count + 2 * SHIFT_H, TILE, width)
    id_shape = (row_count, levels, col_count)
    hbm = pl.BlockSpec(memory_space=pltpu.HBM)
    updated = pl.pallas_call(
        lambda *refs: kernel(n_lon, n_lat, *refs),
        out_shape=pltpu.VMEM(tiles, BF16),
        in_specs=[hbm] * 4,
        out_specs=pl.BlockSpec(memory_space=pltpu.VMEM),
        scratch_shapes=[
            pltpu.VMEM(tiles, BF16),
            pltpu.VMEM(w_qkv.shape, BF16),
            pltpu.VMEM(w_out.shape, BF16),
            pltpu.VMEM(id_shape, jnp.int32),
            pltpu.VMEM((2,) + half, BF16),
            pltpu.VMEM(side, BF16),
            pltpu.VMEM(side, BF16),
            pltpu.VMEM((len(WAYS),) + id_shape, jnp.int32),
            pltpu.VMEM(tiles, F32),
            pltpu.VMEM(tiles, F32),
            pltpu.VMEM(tiles, F32),
            pltpu.SemaphoreType.DMA((4,)),
            pltpu.SemaphoreType.DMA((2 * len(WAYS), 2)),
            pltpu.SemaphoreType.DMA((len(WAYS), 2)),
            pltpu.SemaphoreType.REGULAR((4,)),
        ],
        compiler_params=pltpu.CompilerParams(
            collective_id=0, has_side_effects=True, vmem_limit_bytes=60 * 2**20
        ),
    )(patches.reshape(tiles), regions.transpose(1, 0, 2), w_qkv, w_out)
    return updated.reshape(patches.shape)


def solution(mesh):
    n_lon, n_lat = mesh.shape["lon"], mesh.shape["lat"]
    return jax.shard_map(
        lambda *arrays: shards(n_lon, n_lat, *arrays),
        mesh=mesh,
        in_specs=(P(None, "lat", "lon", None), P(None, "lat", "lon"), P(), P()),
        out_specs=P(None, "lat", "lon", None),
        check_vma=False,
    )
```

```python
import math

import jax
import jax.numpy as jnp
from jax import lax
from jax.experimental import pallas as pl
from jax.experimental.pallas import tpu as pltpu
from jax.sharding import PartitionSpec as P

HEADS = 16
WIN_H = 6
WIN_W = 12
SHIFT_H = 3
SHIFT_W = 6
LEVELS = 2
TILE = 8
GROUP = 4
MESH = pl.DeviceIdType.MESH
F32 = jnp.float32
BF16 = jnp.bfloat16

EAST, EAST_N, EAST_S = 0, 1, 2
WEST, WEST_N, WEST_S = 3, 4, 5
NORTH, SOUTH = 6, 7
WAYS = ((1, 0), (1, -1), (1, 1), (-1, 0), (-1, -1), (-1, 1), (0, -1), (0, 1))
EASTWARD = (EAST, EAST_N, EAST_S)
WESTWARD = (WEST, WEST_N, WEST_S)


def attend(queries, key_vecs, values, bias):
    width = queries.shape[1]
    key_count = key_vecs.shape[0]
    head_depth = width // HEADS
    scale = math.log2(math.e) / math.sqrt(head_depth)
    lane = lax.broadcasted_iota(jnp.int32, (1, 128), 1) // head_depth
    only = [(lane == head).astype(F32).astype(BF16) for head in range(GROUP)]
    ones = jnp.concatenate([jnp.broadcast_to(mask, (key_count, 128)) for mask in only], axis=0)
    sums, totals = [], []
    for group in range(width // 128):
        part = slice(group * 128, (group + 1) * 128)
        scores = lax.dot_general(
            queries[:, part],
            jnp.concatenate([key_vecs[:, part] * mask for mask in only], axis=0),
            (((1,), (1,)), ((), ())),
            preferred_element_type=F32,
        )
        weights = jnp.exp2(scores * scale + bias).astype(BF16)
        spread = jnp.concatenate([values[:, part] * mask for mask in only], axis=0)
        result = jnp.dot(
            weights, jnp.concatenate([spread, ones], axis=1), preferred_element_type=F32
        )
        sums.append(result[:, :128])
        totals.append(result[:, 128:])
    return jnp.concatenate(sums, axis=1), jnp.concatenate(totals, axis=1)


def bias_of(query_code, key_code):
    return jnp.where(query_code == key_code, F32(-8.0), F32(-1e30))


def row_code(ids, shape, dim, cols):
    col = lax.broadcasted_iota(jnp.int32, shape, dim) % cols
    code = jnp.broadcast_to(ids[0], shape)
    for block in range(1, 4):
        code = jnp.where(col >= block * SHIFT_W, ids[block] + 4 * ((block + 1) // 2), code)
    return code


def kernel(
    n_lon, n_lat,
    x_hbm, ids_hbm, w_qkv_hbm, w_out_hbm,
    out_ref,
    x, w_qkv, w_out, ids, beside, east, west, halo_ids, w_sums, queries, sums, totals,
    load_sem, send_sem, recv_sem, ready,
):
    lon, lat = lax.axis_index("lon"), lax.axis_index("lat")
    first, last, before = lon == 0, lon == n_lon - 1, lon == n_lon - 2
    even = lax.rem(lon, 2) == 0
    odd = jnp.logical_not(even)
    crossed_west = jnp.logical_and(even, jnp.logical_not(first))
    north, south = beside.at[0], beside.at[1]

    def east_first(lon):
        late_corner = jnp.logical_and(lon == 0, lat == 0)
        falling = jnp.logical_and(lax.rem(lon, 4) == 3, lon >= n_lon // 2)
        return (lon >= n_lon - 2) | (lon < 0) | late_corner | falling

    def south_first(lat):
        late_corner = jnp.logical_and(lat == 0, lon == 0)
        return jnp.logical_or(lax.rem(lat, n_lat // 2) == n_lat // 2 - 1, late_corner)

    has_north, has_south = lat > 0, lat < n_lat - 1
    more_north, more_south = jnp.where(has_north, 1, 0), jnp.where(has_south, 1, 0)
    three = 1 + more_north + more_south
    width = x.shape[-1]
    half_tokens = LEVELS * SHIFT_H * 3 * TILE

    def device(dlon, dlat):
        return {"lon": lax.rem(lon + dlon + n_lon, n_lon), "lat": lax.rem(lat + dlat + n_lat, n_lat)}

    def exists(way):
        dlat = WAYS[way][1]
        return has_north if dlat < 0 else has_south if dlat > 0 else None

    def comes(way):
        dlat = WAYS[way][1]
        return has_south if dlat < 0 else has_north if dlat > 0 else None

    def when(condition, do):
        def run():
            do()

        if condition is None:
            run()
        else:
            pl.when(condition)(run)

    def signal_all(semaphore, ways):
        for way in ways:
            when(
                exists(way),
                lambda way=way: pl.semaphore_signal(
                    semaphore, inc=1, device_id=device(*WAYS[way]), device_id_type=MESH
                ),
            )

    def message(way, sources, send_index, target):
        dlon, dlat = WAYS[way]
        side = west if dlon > 0 else east
        if dlon == 0:
            landing = south if dlat < 0 else north
        else:
            landing = side.at[0] if dlat == 0 else side.at[1, :, pl.ds(3 if dlat < 0 else 0, 3)]
        return [
            pltpu.make_async_remote_copy(
                src_ref=source,
                dst_ref=place,
                send_sem=send_sem.at[send_index, part],
                recv_sem=recv_sem.at[way, part],
                device_id=device(*target),
                device_id_type=MESH,
            )
            for part, (source, place) in enumerate(zip(sources, (landing, halo_ids.at[way])))
        ]

    def direct(way):
        dlon, dlat = WAYS[way]
        rows = {0: pl.ds(0, 6), -1: pl.ds(0, 3), 1: pl.ds(3, 3)}[dlat]
        source = x_hbm.at[:, rows] if dlon == 0 else x_hbm.at[:, rows, 2 if dlon > 0 else 0]
        return message(way, (source, ids_hbm), way, WAYS[way])

    def send(ways):
        for way in ways:
            when(exists(way), lambda way=way: [copy.start() for copy in direct(way)])

    def wait_recv(ways):
        for way in ways:
            when(comes(way), lambda way=way: [copy.wait_recv() for copy in direct(way)])

    def wait_send(ways):
        for way in ways:
            when(exists(way), lambda way=way: [copy.wait_send() for copy in direct(way)])

    def chip_relays(way):
        source, edge = (north, has_north) if way == SOUTH else (south, has_south)
        to_east, to_west = (EAST_S, WEST_S) if way == SOUTH else (EAST_N, WEST_N)
        return [
            (
                jnp.logical_and(edge, even if dlon > 0 else odd),
                message(to, (source.at[:, :, 2 if dlon > 0 else 0], halo_ids.at[way]), to, (dlon, 0)),
            )
            for to, dlon in ((to_east, 1), (to_west, -1))
        ]

    def lat_relays(way):
        source = west if way == EAST else east
        parts = (
            (EAST_N if way == EAST else WEST_N, has_north, pl.ds(0, 3), -1),
            (EAST_S if way == EAST else WEST_S, has_south, pl.ds(3, 3), 1),
        )
        crossed = crossed_west if way == EAST else odd
        return [
            (
                jnp.logical_and(edge, crossed),
                message(to, (source.at[0, :, rows], halo_ids.at[way]), len(WAYS) + to, (0, dlat)),
            )
            for to, edge, rows, dlat in parts
        ]

    def start(relays):
        for condition, copies in relays:
            when(condition, lambda copies=copies: [copy.start() for copy in copies])

    def finish_relays(relays):
        for condition, copies in relays:
            when(condition, lambda copies=copies: [copy.wait_send() for copy in copies])

    barrier = pltpu.get_barrier_semaphore()
    ready_east, ready_west, ready_north, ready_south = [ready.at[index] for index in range(4)]
    to_east = jnp.logical_or(before, last)
    not_last = jnp.logical_not(last)
    early_east, early_west = east_first(lon), jnp.logical_not(east_first(lon - 1))
    late_east, late_west = jnp.logical_not(early_east), jnp.logical_not(early_west)
    inner_south = jnp.logical_and(has_south, not_last)
    inner_north = jnp.logical_and(has_north, not_last)
    early_south = jnp.logical_and(inner_south, south_first(lat))
    late_south = jnp.logical_and(inner_south, jnp.logical_not(south_first(lat)))
    early_north = jnp.logical_and(inner_north, jnp.logical_not(south_first(lat - 1)))
    late_north = jnp.logical_and(inner_north, south_first(lat - 1))
    seam = jnp.logical_or(first, last)

    pl.when(late_east)(lambda: signal_all(barrier, (EAST,)))
    pl.when(jnp.logical_and(late_west, jnp.logical_not(seam)))(lambda: signal_all(barrier, (WEST,)))
    pl.when(seam)(lambda: signal_all(barrier, WESTWARD))
    pl.when(late_south)(lambda: signal_all(barrier, (SOUTH,)))
    pl.when(late_north)(lambda: signal_all(barrier, (NORTH,)))

    loads = [
        pltpu.make_async_copy(source, target, load_sem.at[index])
        for index, (source, target) in enumerate(
            ((x_hbm, x), (ids_hbm, ids), (w_qkv_hbm, w_qkv), (w_out_hbm, w_out))
        )
    ]

    def start_loads():
        for load in loads:
            load.start()

    pl.when(not_last)(start_loads)
    greeted = (
        jnp.where(early_west, 1, 0)
        + jnp.where(early_east, jnp.where(to_east, three, 1), 0)
        + jnp.where(jnp.logical_or(early_north, early_south), 1, 0)
        + jnp.where(jnp.logical_and(early_north, early_south), 1, 0)
    )

    @pl.when(greeted > 0)
    def _():
        pl.semaphore_wait(barrier, greeted)

    @pl.when(last)
    def _():
        signal_all(ready_west, (EAST,))
        send((EAST_N, EAST_S, EAST))
        start_loads()

    inner_east = jnp.logical_and(early_east, not_last)
    pl.when(early_north)(lambda: signal_all(ready_south, (NORTH,)))
    pl.when(early_south)(lambda: signal_all(ready_north, (SOUTH,)))
    pl.when(early_west)(lambda: signal_all(ready_east, (WEST,)))
    pl.when(inner_east)(lambda: signal_all(ready_west, (EAST,)))
    pl.when(early_west)(lambda: send((WEST,)))
    pl.when(early_south)(lambda: send((SOUTH,)))
    pl.when(early_north)(lambda: send((NORTH,)))
    pl.when(inner_east)(lambda: send((EAST,)))

    @pl.when(jnp.logical_not(has_north))
    def _():
        east[1, :, 0:3] = jnp.zeros((LEVELS, 3, TILE, width), BF16)
        west[1, :, 0:3] = jnp.zeros((LEVELS, 3, TILE, width), BF16)
        for way in (EAST_S, WEST_S):
            halo_ids[way] = jnp.zeros(halo_ids.shape[1:], jnp.int32)

    @pl.when(jnp.logical_not(has_south))
    def _():
        east[1, :, 3:6] = jnp.zeros((LEVELS, 3, TILE, width), BF16)
        west[1, :, 3:6] = jnp.zeros((LEVELS, 3, TILE, width), BF16)
        for way in (EAST_N, WEST_N):
            halo_ids[way] = jnp.zeros(halo_ids.shape[1:], jnp.int32)

    def class_of(ref, row, block):
        return ref[row, 0:1, block * SHIFT_W : block * SHIFT_W + 1]

    def classes(ref, row):
        return [class_of(ref, row, block) for block in range(4)]

    def query_code(half):
        return row_code(classes(ids, 3 * half), (half_tokens, 1), 0, 24)

    def project(source, first_feature):
        values = source.astype(F32).reshape(-1, width)
        center = jnp.mean(values, axis=-1, keepdims=True)
        spread = jnp.mean(jnp.square(values - center), axis=-1, keepdims=True)
        product = jnp.dot(
            values.astype(BF16), w_qkv[:, first_feature:], preferred_element_type=F32
        )
        return (product - center * w_sums[0:1, first_feature:]) * lax.rsqrt(spread + 1e-05)

    def project_halo(source):
        both = project(source, width).astype(BF16)
        return both[:, :width], both[:, width:]

    for load in loads[:3]:
        load.wait()
    block = (LEVELS, 3, 3, TILE, width)
    w_sums[...] = jnp.dot(
        jnp.ones((TILE, width), BF16), w_qkv[...], preferred_element_type=F32
    )
    for half in range(2):
        rows = slice(3 * half, 3 * half + 3)
        projected = project(x[:, rows], 0)
        queries[:, rows] = projected[:, :width].reshape(block)
        projected = projected.astype(BF16)
        key_code = row_code(classes(ids, 3 * half), (1, GROUP * half_tokens), 1, 24)
        some, total = attend(
            projected[:, :width],
            projected[:, width : 2 * width],
            projected[:, 2 * width :],
            bias_of(query_code(half), key_code),
        )
        sums[:, rows] = some.reshape(block)
        totals[:, rows] = total.reshape(block)
        if half == 0:

            @pl.when(late_south)
            def _():
                pl.semaphore_wait(ready_south, 1)
                send((SOUTH,))

            @pl.when(last)
            def _():
                pl.semaphore_wait(ready_west, 1)
                send((NORTH, SOUTH, WEST))

    @pl.when(late_east)
    def _():
        pl.semaphore_wait(ready_east, 1)
        send((EAST,))

    @pl.when(late_north)
    def _():
        pl.semaphore_wait(ready_north, 1)
        send((NORTH,))

    @pl.when(jnp.logical_and(late_west, jnp.logical_not(seam)))
    def _():
        pl.semaphore_wait(ready_west, 1)
        send((WEST,))

    def row_halo(half):
        rows = pl.ds(3 * half, 3)
        key_vecs, values = project_halo(beside[half])
        their_ids = halo_ids.at[jnp.where(half == 0, SOUTH, NORTH)]
        key_code = row_code(classes(their_ids, 3 - 3 * half), (1, GROUP * half_tokens), 1, 24)
        some, total = attend(
            queries[:, rows].reshape(half_tokens, width).astype(BF16),
            key_vecs,
            values,
            bias_of(query_code(half), key_code),
        )
        sums[:, rows] += some.reshape(block)
        totals[:, rows] += total.reshape(block)

    def side_halo(tile, source, part, ways, query_block, key_block, query_cols, key_cols):
        straight, from_south, from_north = ways
        key_vecs, values = project_halo(source[part])
        shape = (LEVELS * 6 * TILE, 1)
        token = lax.broadcasted_iota(jnp.int32, shape, 0)
        col, row = token % TILE, token // TILE % 6
        mine = jnp.where(
            row >= 3, class_of(ids, 3, query_block) + 4, class_of(ids, 0, query_block)
        )
        mine = jnp.where((col >= query_cols[0]) & (col < query_cols[1]), mine, -2)
        token = lax.broadcasted_iota(jnp.int32, (1, GROUP * shape[0]), 1)
        col, row = token % TILE, token // TILE % 6
        corner = part == 1
        upper = halo_ids.at[jnp.where(corner, from_north, straight)]
        lower = halo_ids.at[jnp.where(corner, from_south, straight)]
        theirs = jnp.where(
            row >= 3,
            class_of(lower, jnp.where(corner, 0, 3), key_block) + 4,
            class_of(upper, jnp.where(corner, 3, 0), key_block),
        )
        seen = (col >= key_cols[0]) & (col < key_cols[1])
        seen = seen & (row >= jnp.where(corner, 3 * (1 - more_north), 0))
        seen = seen & (row < jnp.where(corner, 3 + 3 * more_south, 6))
        some, total = attend(
            queries[:, :, tile].reshape(-1, width).astype(BF16),
            key_vecs,
            values,
            bias_of(mine, jnp.where(seen, theirs, -1)),
        )
        side = (LEVELS, 6, TILE, width)
        sums[:, :, tile] += some.reshape(side)
        totals[:, :, tile] += total.reshape(side)

    def east_halo(part):
        side_halo(2, east, part, WESTWARD, 3, 0, (2, 8), (0, 6))

    def west_halo(part):
        side_halo(0, west, part, EASTWARD, 0, 3, (0, 6), (2, 8))

    def finish(tiles):
        attended = (sums[:, :, tiles] / totals[:, :, tiles]).astype(BF16).reshape(-1, width)
        output = jnp.dot(attended, w_out[...], preferred_element_type=F32)
        patches = x[:, :, tiles].astype(F32)
        out_ref[:, :, tiles] = (patches + output.reshape(patches.shape)).astype(BF16)

    def relay_east():
        wait_recv((WEST,))
        start(lat_relays(WEST))

    def relay_west():
        wait_recv((EAST,))
        start(lat_relays(EAST))

    north_first = jnp.where(early_south | (last & south_first(lat)), 1, 0)
    for step in range(2):
        half = 1 - north_first if step == 0 else north_first
        if step == 0:
            pl.when(jnp.logical_and(odd, not_last))(relay_east)

        @pl.when(half == 0)
        def _():
            wait_recv((SOUTH,))
            start(chip_relays(SOUTH))

        @pl.when(half == 1)
        def _():
            wait_recv((NORTH,))
            start(chip_relays(NORTH))

        if step == 0:
            pl.when(crossed_west)(relay_west)

        @pl.when(jnp.where(half == 0, more_north, more_south) == 1)
        def _():
            row_halo(half)

        if step == 0:

            @pl.when(odd)
            def _():
                wait_recv((EAST,))

            pl.when(jnp.logical_not(first))(lambda: west_halo(0))

            @pl.when(even)
            def _():
                wait_recv((WEST,))

            pl.when(last)(relay_east)
            east_halo(0)

    @pl.when(first)
    def _():
        pl.semaphore_wait(ready_west, 1)
        send((WEST,))

    wait_recv((WEST_N, WEST_S))
    east_halo(1)
    loads[3].wait()
    finish(slice(1, 3))
    straight_first = first & has_north & (lax.rem(lat, n_lat // 2) == 0)
    corners_first = jnp.logical_not(straight_first)

    @pl.when(straight_first)
    def _():
        wait_recv((EAST,))

    @pl.when(corners_first)
    def _():
        wait_recv((EAST_N, EAST_S))

    pl.when(first)(lambda: west_halo(jnp.where(straight_first, 0, 1)))

    @pl.when(straight_first)
    def _():
        wait_recv((EAST_N, EAST_S))

    @pl.when(jnp.logical_and(first, corners_first))
    def _():
        wait_recv((EAST,))

    west_halo(jnp.where(jnp.logical_and(first, corners_first), 0, 1))
    finish(slice(0, 1))

    wait_send((EAST, WEST, NORTH, SOUTH))

    @pl.when(last)
    def _():
        wait_send((EAST_N, EAST_S))

    for way in (NORTH, SOUTH):
        finish_relays(chip_relays(way))
    for way in (EAST, WEST):
        finish_relays(lat_relays(way))


def shards(n_lon, n_lat, patches, regions, w_qkv, w_out):
    levels, row_count, col_count, width = patches.shape
    tiles = (levels, row_count, col_count // TILE, TILE, width)
    half = (levels, SHIFT_H, col_count // TILE, TILE, width)
    side = (2, levels, row_count, TILE, width)
    id_shape = (row_count, levels, col_count)
    hbm = pl.BlockSpec(memory_space=pltpu.HBM)
    updated = pl.pallas_call(
        lambda *refs: kernel(n_lon, n_lat, *refs),
        out_shape=pltpu.VMEM(tiles, BF16),
        in_specs=[hbm] * 4,
        out_specs=pl.BlockSpec(memory_space=pltpu.VMEM),
        scratch_shapes=[
            pltpu.VMEM(tiles, BF16),
            pltpu.VMEM(w_qkv.shape, BF16),
            pltpu.VMEM(w_out.shape, BF16),
            pltpu.VMEM(id_shape, jnp.int32),
            pltpu.VMEM((2,) + half, BF16),
            pltpu.VMEM(side, BF16),
            pltpu.VMEM(side, BF16),
            pltpu.VMEM((len(WAYS),) + id_shape, jnp.int32),
            pltpu.VMEM((TILE, w_qkv.shape[1]), F32),
            pltpu.VMEM(tiles, F32),
            pltpu.VMEM(tiles, F32),
            pltpu.VMEM(tiles, F32),
            pltpu.SemaphoreType.DMA((4,)),
            pltpu.SemaphoreType.DMA((2 * len(WAYS), 2)),
            pltpu.SemaphoreType.DMA((len(WAYS), 2)),
            pltpu.SemaphoreType.REGULAR((4,)),
        ],
        compiler_params=pltpu.CompilerParams(
            collective_id=0, has_side_effects=True, vmem_limit_bytes=60 * 2**20
        ),
    )(patches.reshape(tiles), regions.transpose(1, 0, 2), w_qkv, w_out)
    return updated.reshape(patches.shape)


def solution(mesh):
    n_lon, n_lat = mesh.shape["lon"], mesh.shape["lat"]
    return jax.shard_map(
        lambda *arrays: shards(n_lon, n_lat, *arrays),
        mesh=mesh,
        in_specs=(P(None, "lat", "lon", None), P(None, "lat", "lon"), P(), P()),
        out_specs=P(None, "lat", "lon", None),
        check_vma=False,
    )
```

```python
import math

import jax
import jax.numpy as jnp
from jax import lax
from jax.experimental import pallas as pl
from jax.experimental.pallas import tpu as pltpu
from jax.sharding import PartitionSpec as P

HEADS = 16
WIN_H = 6
WIN_W = 12
SHIFT_H = 3
SHIFT_W = 6
LEVELS = 2
TILE = 8
GROUP = 4
MESH = pl.DeviceIdType.MESH
F32 = jnp.float32
BF16 = jnp.bfloat16

EAST, EAST_N, EAST_S = 0, 1, 2
WEST, WEST_N, WEST_S = 3, 4, 5
NORTH, SOUTH = 6, 7
WAYS = ((1, 0), (1, -1), (1, 1), (-1, 0), (-1, -1), (-1, 1), (0, -1), (0, 1))
EASTWARD = (EAST, EAST_N, EAST_S)
WESTWARD = (WEST, WEST_N, WEST_S)


def attend(sets):
    width = sets[0][0].shape[1]
    head_depth = width // HEADS
    scale = math.log2(math.e) / math.sqrt(head_depth)
    lane = lax.broadcasted_iota(jnp.int32, (1, 128), 1) // head_depth
    only = [(lane == head).astype(F32).astype(BF16) for head in range(GROUP)]
    parts = [slice(group * 128, (group + 1) * 128) for group in range(width // 128)]

    def repeated(vectors):
        return jnp.concatenate([vectors * mask for mask in only], axis=0)

    scores = [
        lax.dot_general(
            queries[:, part],
            repeated(key_vecs[:, part]),
            (((1,), (1,)), ((), ())),
            preferred_element_type=F32,
        )
        for queries, key_vecs, _, _ in sets
        for part in parts
    ]
    weights = [
        jnp.exp2(score * scale + sets[index // len(parts)][3]).astype(BF16)
        for index, score in enumerate(scores)
    ]
    found = []
    for index, (_, key_vecs, values, _) in enumerate(sets):
        ones = repeated(jnp.ones((key_vecs.shape[0], 128), BF16))
        results = [
            jnp.dot(
                weights[index * len(parts) + group],
                jnp.concatenate([repeated(values[:, part]), ones], axis=1),
                preferred_element_type=F32,
            )
            for group, part in enumerate(parts)
        ]
        found.append(
            (
                jnp.concatenate([result[:, :128] for result in results], axis=1),
                jnp.concatenate([result[:, 128:] for result in results], axis=1),
            )
        )
    return found


def bias_of(query_code, key_code):
    return jnp.where(query_code == key_code, F32(-8.0), F32(-1e30))


def row_code(ids, shape, dim, cols):
    col = lax.broadcasted_iota(jnp.int32, shape, dim) % cols
    code = jnp.broadcast_to(ids[0], shape)
    for block in range(1, 4):
        code = jnp.where(col >= block * SHIFT_W, ids[block] + 4 * ((block + 1) // 2), code)
    return code


def kernel(
    n_lon, n_lat,
    x_hbm, ids_hbm, w_qkv_hbm, w_out_hbm,
    out_ref,
    x, w_qkv, w_out, ids, beside, east, west, halo_ids, w_sums, queries, sums, totals,
    load_sem, send_sem, recv_sem, ready,
):
    lon, lat = lax.axis_index("lon"), lax.axis_index("lat")
    first, last, before = lon == 0, lon == n_lon - 1, lon == n_lon - 2
    even = lax.rem(lon, 2) == 0
    odd = jnp.logical_not(even)
    crossed_west = jnp.logical_and(even, jnp.logical_not(first))
    north, south = beside.at[0], beside.at[1]

    def east_first(lon):
        late_corner = jnp.logical_and(lon == 0, lat == 0)
        falling = jnp.logical_and(lax.rem(lon, 4) == 3, lon >= n_lon // 2)
        return (lon >= n_lon - 2) | (lon < 0) | late_corner | falling

    def south_first(lat):
        late_corner = jnp.logical_and(lat == 0, lon == 0)
        return jnp.logical_or(lax.rem(lat, n_lat // 2) == n_lat // 2 - 1, late_corner)

    has_north, has_south = lat > 0, lat < n_lat - 1
    more_north, more_south = jnp.where(has_north, 1, 0), jnp.where(has_south, 1, 0)
    three = 1 + more_north + more_south
    width = x.shape[-1]
    half_tokens = LEVELS * SHIFT_H * 3 * TILE

    def device(dlon, dlat):
        return {"lon": lax.rem(lon + dlon + n_lon, n_lon), "lat": lax.rem(lat + dlat + n_lat, n_lat)}

    def exists(way):
        dlat = WAYS[way][1]
        return has_north if dlat < 0 else has_south if dlat > 0 else None

    def comes(way):
        dlat = WAYS[way][1]
        return has_south if dlat < 0 else has_north if dlat > 0 else None

    def when(condition, do):
        def run():
            do()

        if condition is None:
            run()
        else:
            pl.when(condition)(run)

    def signal_all(semaphore, ways):
        for way in ways:
            when(
                exists(way),
                lambda way=way: pl.semaphore_signal(
                    semaphore, inc=1, device_id=device(*WAYS[way]), device_id_type=MESH
                ),
            )

    def message(way, sources, send_index, target):
        dlon, dlat = WAYS[way]
        side = west if dlon > 0 else east
        if dlon == 0:
            landing = south if dlat < 0 else north
        else:
            landing = side.at[0] if dlat == 0 else side.at[1, :, pl.ds(3 if dlat < 0 else 0, 3)]
        return [
            pltpu.make_async_remote_copy(
                src_ref=source,
                dst_ref=place,
                send_sem=send_sem.at[send_index, part],
                recv_sem=recv_sem.at[way, part],
                device_id=device(*target),
                device_id_type=MESH,
            )
            for part, (source, place) in enumerate(zip(sources, (landing, halo_ids.at[way])))
        ]

    def direct(way):
        dlon, dlat = WAYS[way]
        rows = {0: pl.ds(0, 6), -1: pl.ds(0, 3), 1: pl.ds(3, 3)}[dlat]
        source = x_hbm.at[:, rows] if dlon == 0 else x_hbm.at[:, rows, 2 if dlon > 0 else 0]
        return message(way, (source, ids_hbm), way, WAYS[way])

    def send(ways):
        for way in ways:
            when(exists(way), lambda way=way: [copy.start() for copy in direct(way)])

    def wait_recv(ways):
        for way in ways:
            when(comes(way), lambda way=way: [copy.wait_recv() for copy in direct(way)])

    def wait_send(ways):
        for way in ways:
            when(exists(way), lambda way=way: [copy.wait_send() for copy in direct(way)])

    def chip_relays(way):
        source, edge = (north, has_north) if way == SOUTH else (south, has_south)
        to_east, to_west = (EAST_S, WEST_S) if way == SOUTH else (EAST_N, WEST_N)
        return [
            (
                jnp.logical_and(edge, even if dlon > 0 else odd),
                message(to, (source.at[:, :, 2 if dlon > 0 else 0], halo_ids.at[way]), to, (dlon, 0)),
            )
            for to, dlon in ((to_east, 1), (to_west, -1))
        ]

    def lat_relays(way):
        source = west if way == EAST else east
        parts = (
            (EAST_N if way == EAST else WEST_N, has_north, pl.ds(0, 3), -1),
            (EAST_S if way == EAST else WEST_S, has_south, pl.ds(3, 3), 1),
        )
        crossed = crossed_west if way == EAST else odd
        return [
            (
                jnp.logical_and(edge, crossed),
                message(to, (source.at[0, :, rows], halo_ids.at[way]), len(WAYS) + to, (0, dlat)),
            )
            for to, edge, rows, dlat in parts
        ]

    def start(relays):
        for condition, copies in relays:
            when(condition, lambda copies=copies: [copy.start() for copy in copies])

    def finish_relays(relays):
        for condition, copies in relays:
            when(condition, lambda copies=copies: [copy.wait_send() for copy in copies])

    barrier = pltpu.get_barrier_semaphore()
    ready_east, ready_west, ready_north, ready_south = [ready.at[index] for index in range(4)]
    to_east = jnp.logical_or(before, last)
    not_last = jnp.logical_not(last)
    early_east, early_west = east_first(lon), jnp.logical_not(east_first(lon - 1))
    late_east, late_west = jnp.logical_not(early_east), jnp.logical_not(early_west)
    inner_south = jnp.logical_and(has_south, not_last)
    inner_north = jnp.logical_and(has_north, not_last)
    early_south = jnp.logical_and(inner_south, south_first(lat))
    late_south = jnp.logical_and(inner_south, jnp.logical_not(south_first(lat)))
    early_north = jnp.logical_and(inner_north, jnp.logical_not(south_first(lat - 1)))
    late_north = jnp.logical_and(inner_north, south_first(lat - 1))
    seam = jnp.logical_or(first, last)

    pl.when(late_east)(lambda: signal_all(barrier, (EAST,)))
    pl.when(jnp.logical_and(late_west, jnp.logical_not(seam)))(lambda: signal_all(barrier, (WEST,)))
    pl.when(seam)(lambda: signal_all(barrier, WESTWARD))
    pl.when(late_south)(lambda: signal_all(barrier, (SOUTH,)))
    pl.when(late_north)(lambda: signal_all(barrier, (NORTH,)))

    loads = [
        pltpu.make_async_copy(source, target, load_sem.at[index])
        for index, (source, target) in enumerate(
            ((x_hbm, x), (ids_hbm, ids), (w_qkv_hbm, w_qkv), (w_out_hbm, w_out))
        )
    ]

    def start_loads():
        for load in loads:
            load.start()

    pl.when(not_last)(start_loads)
    greeted = (
        jnp.where(early_west, 1, 0)
        + jnp.where(early_east, jnp.where(to_east, three, 1), 0)
        + jnp.where(jnp.logical_or(early_north, early_south), 1, 0)
        + jnp.where(jnp.logical_and(early_north, early_south), 1, 0)
    )

    @pl.when(greeted > 0)
    def _():
        pl.semaphore_wait(barrier, greeted)

    @pl.when(last)
    def _():
        signal_all(ready_west, (EAST,))
        send((EAST_N, EAST_S, EAST))
        start_loads()

    inner_east = jnp.logical_and(early_east, not_last)
    pl.when(early_north)(lambda: signal_all(ready_south, (NORTH,)))
    pl.when(early_south)(lambda: signal_all(ready_north, (SOUTH,)))
    pl.when(early_west)(lambda: signal_all(ready_east, (WEST,)))
    pl.when(inner_east)(lambda: signal_all(ready_west, (EAST,)))
    pl.when(early_west)(lambda: send((WEST,)))
    pl.when(early_south)(lambda: send((SOUTH,)))
    pl.when(early_north)(lambda: send((NORTH,)))
    pl.when(inner_east)(lambda: send((EAST,)))

    @pl.when(jnp.logical_not(has_north))
    def _():
        east[1, :, 0:3] = jnp.zeros((LEVELS, 3, TILE, width), BF16)
        west[1, :, 0:3] = jnp.zeros((LEVELS, 3, TILE, width), BF16)
        for way in (EAST_S, WEST_S):
            halo_ids[way] = jnp.zeros(halo_ids.shape[1:], jnp.int32)

    @pl.when(jnp.logical_not(has_south))
    def _():
        east[1, :, 3:6] = jnp.zeros((LEVELS, 3, TILE, width), BF16)
        west[1, :, 3:6] = jnp.zeros((LEVELS, 3, TILE, width), BF16)
        for way in (EAST_N, WEST_N):
            halo_ids[way] = jnp.zeros(halo_ids.shape[1:], jnp.int32)

    def class_of(ref, row, block):
        return ref[row, 0:1, block * SHIFT_W : block * SHIFT_W + 1]

    def classes(ref, row):
        return [class_of(ref, row, block) for block in range(4)]

    def query_code(half):
        return row_code(classes(ids, 3 * half), (half_tokens, 1), 0, 24)

    def project(source, first_feature):
        values = source.astype(F32).reshape(-1, width)
        center = jnp.mean(values, axis=-1, keepdims=True)
        spread = jnp.mean(jnp.square(values - center), axis=-1, keepdims=True)
        product = jnp.dot(
            values.astype(BF16), w_qkv[:, first_feature:], preferred_element_type=F32
        )
        return (product - center * w_sums[0:1, first_feature:]) * lax.rsqrt(spread + 1e-05)

    for load in loads[:3]:
        load.wait()
    block = (LEVELS, 3, 3, TILE, width)
    w_sums[...] = jnp.dot(
        jnp.ones((TILE, width), BF16), w_qkv[...], preferred_element_type=F32
    )
    for half in range(2):
        rows = slice(3 * half, 3 * half + 3)
        projected = project(x[:, rows], 0)
        queries[:, rows] = projected[:, :width].reshape(block)
        projected = projected.astype(BF16)
        key_code = row_code(classes(ids, 3 * half), (1, GROUP * half_tokens), 1, 24)
        ((some, total),) = attend(
            [
                (
                    projected[:, :width],
                    projected[:, width : 2 * width],
                    projected[:, 2 * width :],
                    bias_of(query_code(half), key_code),
                )
            ]
        )
        sums[:, rows] = some.reshape(block)
        totals[:, rows] = total.reshape(block)
        if half == 0:

            @pl.when(late_south)
            def _():
                pl.semaphore_wait(ready_south, 1)
                send((SOUTH,))

            @pl.when(last)
            def _():
                pl.semaphore_wait(ready_west, 1)
                send((NORTH, SOUTH, WEST))

    @pl.when(late_east)
    def _():
        pl.semaphore_wait(ready_east, 1)
        send((EAST,))

    @pl.when(late_north)
    def _():
        pl.semaphore_wait(ready_north, 1)
        send((NORTH,))

    @pl.when(jnp.logical_and(late_west, jnp.logical_not(seam)))
    def _():
        pl.semaphore_wait(ready_west, 1)
        send((WEST,))

    def row_halo(half):
        rows = pl.ds(3 * half, 3)
        both = project(beside[half], width).astype(BF16)
        key_vecs, values = both[:, :width], both[:, width:]
        their_ids = halo_ids.at[jnp.where(half == 0, SOUTH, NORTH)]
        key_code = row_code(classes(their_ids, 3 - 3 * half), (1, GROUP * half_tokens), 1, 24)
        ((some, total),) = attend(
            [
                (
                    queries[:, rows].reshape(half_tokens, width).astype(BF16),
                    key_vecs,
                    values,
                    bias_of(query_code(half), key_code),
                )
            ]
        )
        sums[:, rows] += some.reshape(block)
        totals[:, rows] += total.reshape(block)

    def side_halo(tile, source, part, ways, query_block, key_block, query_cols, key_cols):
        straight, from_south, from_north = ways
        corner = part == 1
        tokens = LEVELS * 3 * TILE
        side = (LEVELS, 3, TILE, width)
        both = project(source[part], width).reshape(LEVELS, 6, TILE, 2 * width)
        query_col = lax.broadcasted_iota(jnp.int32, (tokens, 1), 0) % TILE
        key_col = lax.broadcasted_iota(jnp.int32, (1, GROUP * tokens), 1) % TILE
        sets = []
        for half, way, exists_there in ((0, from_north, more_north), (1, from_south, more_south)):
            rows = slice(3 * half, 3 * half + 3)
            there = halo_ids.at[jnp.where(corner, way, straight)]
            theirs = class_of(there, jnp.where(corner, 3 - 3 * half, 3 * half), key_block)
            theirs = jnp.where(jnp.logical_and(corner, exists_there == 0), -1, theirs)
            key_code = jnp.where((key_col >= key_cols[0]) & (key_col < key_cols[1]), theirs, -1)
            mine = class_of(ids, 3 * half, query_block)
            in_window = (query_col >= query_cols[0]) & (query_col < query_cols[1])
            vectors = both[:, rows].reshape(tokens, 2 * width).astype(BF16)
            sets.append(
                (
                    queries[:, rows, tile].reshape(tokens, width).astype(BF16),
                    vectors[:, :width],
                    vectors[:, width:],
                    bias_of(jnp.where(in_window, mine, -2), key_code),
                )
            )
        for half, (some, total) in enumerate(attend(sets)):
            rows = slice(3 * half, 3 * half + 3)
            sums[:, rows, tile] += some.reshape(side)
            totals[:, rows, tile] += total.reshape(side)

    def east_halo(part):
        side_halo(2, east, part, WESTWARD, 3, 0, (2, 8), (0, 6))

    def west_halo(part):
        side_halo(0, west, part, EASTWARD, 0, 3, (0, 6), (2, 8))

    def finish(tiles):
        attended = (sums[:, :, tiles] / totals[:, :, tiles]).astype(BF16).reshape(-1, width)
        output = jnp.dot(attended, w_out[...], preferred_element_type=F32)
        patches = x[:, :, tiles].astype(F32)
        out_ref[:, :, tiles] = (patches + output.reshape(patches.shape)).astype(BF16)

    def relay_east():
        wait_recv((WEST,))
        start(lat_relays(WEST))

    def relay_west():
        wait_recv((EAST,))
        start(lat_relays(EAST))

    north_first = jnp.where(early_south | (last & south_first(lat)), 1, 0)
    for step in range(2):
        half = 1 - north_first if step == 0 else north_first
        if step == 0:
            pl.when(jnp.logical_and(odd, not_last))(relay_east)
            pl.when(jnp.logical_and(crossed_west, north_first == 1))(relay_west)

        @pl.when(half == 0)
        def _():
            wait_recv((SOUTH,))
            start(chip_relays(SOUTH))

        @pl.when(half == 1)
        def _():
            wait_recv((NORTH,))
            start(chip_relays(NORTH))

        @pl.when(jnp.where(half == 0, more_north, more_south) == 1)
        def _():
            row_halo(half)

        if step == 0:

            @pl.when(even)
            def _():
                wait_recv((WEST,))

            pl.when(not_last)(lambda: east_halo(0))
            pl.when(jnp.logical_and(crossed_west, north_first == 0))(relay_west)

            @pl.when(odd)
            def _():
                wait_recv((EAST,))

            pl.when(jnp.logical_not(first))(lambda: west_halo(0))

            @pl.when(last)
            def _():
                relay_east()
                east_halo(0)

    @pl.when(first)
    def _():
        pl.semaphore_wait(ready_west, 1)
        send((WEST,))

    wait_recv((WEST_N, WEST_S))
    east_halo(1)
    loads[3].wait()
    finish(slice(1, 3))
    wait_send((EAST, WEST, NORTH, SOUTH))

    @pl.when(last)
    def _():
        wait_send((EAST_N, EAST_S))

    for way in (NORTH, SOUTH):
        finish_relays(chip_relays(way))
    for way in (EAST, WEST):
        finish_relays(lat_relays(way))

    straight_first = first & has_north & (lax.rem(lat, n_lat // 2) == 0)
    corners_first = jnp.logical_not(straight_first)

    @pl.when(straight_first)
    def _():
        wait_recv((EAST,))

    @pl.when(corners_first)
    def _():
        wait_recv((EAST_N, EAST_S))

    pl.when(first)(lambda: west_halo(jnp.where(straight_first, 0, 1)))

    @pl.when(straight_first)
    def _():
        wait_recv((EAST_N, EAST_S))

    @pl.when(jnp.logical_and(first, corners_first))
    def _():
        wait_recv((EAST,))

    west_halo(jnp.where(jnp.logical_and(first, corners_first), 0, 1))
    finish(slice(0, 1))


def shards(n_lon, n_lat, patches, regions, w_qkv, w_out):
    levels, row_count, col_count, width = patches.shape
    tiles = (levels, row_count, col_count // TILE, TILE, width)
    half = (levels, SHIFT_H, col_count // TILE, TILE, width)
    side = (2, levels, row_count, TILE, width)
    id_shape = (row_count, levels, col_count)
    hbm = pl.BlockSpec(memory_space=pltpu.HBM)
    updated = pl.pallas_call(
        lambda *refs: kernel(n_lon, n_lat, *refs),
        out_shape=pltpu.VMEM(tiles, BF16),
        in_specs=[hbm] * 4,
        out_specs=pl.BlockSpec(memory_space=pltpu.VMEM),
        scratch_shapes=[
            pltpu.VMEM(tiles, BF16),
            pltpu.VMEM(w_qkv.shape, BF16),
            pltpu.VMEM(w_out.shape, BF16),
            pltpu.VMEM(id_shape, jnp.int32),
            pltpu.VMEM((2,) + half, BF16),
            pltpu.VMEM(side, BF16),
            pltpu.VMEM(side, BF16),
            pltpu.VMEM((len(WAYS),) + id_shape, jnp.int32),
            pltpu.VMEM((TILE, w_qkv.shape[1]), F32),
            pltpu.VMEM(tiles, F32),
            pltpu.VMEM(tiles, F32),
            pltpu.VMEM(tiles, F32),
            pltpu.SemaphoreType.DMA((4,)),
            pltpu.SemaphoreType.DMA((2 * len(WAYS), 2)),
            pltpu.SemaphoreType.DMA((len(WAYS), 2)),
            pltpu.SemaphoreType.REGULAR((4,)),
        ],
        compiler_params=pltpu.CompilerParams(
            collective_id=0, has_side_effects=True, vmem_limit_bytes=60 * 2**20
        ),
    )(patches.reshape(tiles), regions.transpose(1, 0, 2), w_qkv, w_out)
    return updated.reshape(patches.shape)


def solution(mesh):
    n_lon, n_lat = mesh.shape["lon"], mesh.shape["lat"]
    return jax.shard_map(
        lambda *arrays: shards(n_lon, n_lat, *arrays),
        mesh=mesh,
        in_specs=(P(None, "lat", "lon", None), P(None, "lat", "lon"), P(), P()),
        out_specs=P(None, "lat", "lon", None),
        check_vma=False,
    )
```

```python
import math

import jax
import jax.numpy as jnp
from jax import lax
from jax.experimental import pallas as pl
from jax.experimental.pallas import tpu as pltpu
from jax.sharding import PartitionSpec as P

HEADS = 16
WIN_H = 6
WIN_W = 12
SHIFT_H = 3
SHIFT_W = 6
LEVELS = 2
TILE = 8
GROUP = 4
MESH = pl.DeviceIdType.MESH
F32 = jnp.float32
BF16 = jnp.bfloat16

EAST, EAST_N, EAST_S = 0, 1, 2
WEST, WEST_N, WEST_S = 3, 4, 5
NORTH, SOUTH = 6, 7
WAYS = ((1, 0), (1, -1), (1, 1), (-1, 0), (-1, -1), (-1, 1), (0, -1), (0, 1))
EASTWARD = (EAST, EAST_N, EAST_S)
WESTWARD = (WEST, WEST_N, WEST_S)


def attend(sets):
    width = sets[0][0].shape[1]
    head_depth = width // HEADS
    scale = math.log2(math.e) / math.sqrt(head_depth)
    lane = lax.broadcasted_iota(jnp.int32, (1, 128), 1) // head_depth
    only = [(lane == head).astype(F32).astype(BF16) for head in range(GROUP)]
    parts = [slice(group * 128, (group + 1) * 128) for group in range(width // 128)]

    def repeated(vectors):
        return jnp.concatenate([vectors * mask for mask in only], axis=0)

    scores = [
        lax.dot_general(
            queries[:, part],
            repeated(key_vecs[:, part]),
            (((1,), (1,)), ((), ())),
            preferred_element_type=F32,
        )
        for queries, key_vecs, _, _ in sets
        for part in parts
    ]
    weights = [
        jnp.exp2(score * scale + sets[index // len(parts)][3]).astype(BF16)
        for index, score in enumerate(scores)
    ]
    found = []
    for index, (_, key_vecs, values, _) in enumerate(sets):
        ones = repeated(jnp.ones((key_vecs.shape[0], 128), BF16))
        results = [
            jnp.dot(
                weights[index * len(parts) + group],
                jnp.concatenate([repeated(values[:, part]), ones], axis=1),
                preferred_element_type=F32,
            )
            for group, part in enumerate(parts)
        ]
        found.append(
            (
                jnp.concatenate([result[:, :128] for result in results], axis=1),
                jnp.concatenate([result[:, 128:] for result in results], axis=1),
            )
        )
    return found


def bias_of(query_code, key_code):
    return jnp.where(query_code == key_code, F32(-8.0), F32(-1e30))


def row_code(ids, shape, dim, cols):
    col = lax.broadcasted_iota(jnp.int32, shape, dim) % cols
    code = jnp.broadcast_to(ids[0], shape)
    for block in range(1, 4):
        code = jnp.where(col >= block * SHIFT_W, ids[block] + 4 * ((block + 1) // 2), code)
    return code


def kernel(
    n_lon, n_lat,
    x_hbm, ids_hbm, w_qkv_hbm, w_out_hbm,
    out_ref,
    x, w_qkv, w_out, ids, beside, east, west, halo_ids, w_sums, queries, sums, totals,
    load_sem, send_sem, recv_sem, ready,
):
    lon, lat = lax.axis_index("lon"), lax.axis_index("lat")
    first, last, before = lon == 0, lon == n_lon - 1, lon == n_lon - 2
    even = lax.rem(lon, 2) == 0
    odd = jnp.logical_not(even)
    crossed_west = jnp.logical_and(even, jnp.logical_not(first))
    north, south = beside.at[0], beside.at[1]

    def east_first(lon):
        late_corner = jnp.logical_and(lon == 0, lat == 0)
        falling = jnp.logical_and(lax.rem(lon, 4) == 3, lon >= n_lon // 2)
        return (lon >= n_lon - 2) | (lon < 0) | late_corner | falling

    def south_first(lat):
        late_corner = jnp.logical_and(lat == 0, lon == 0)
        return jnp.logical_or(lax.rem(lat, n_lat // 2) == n_lat // 2 - 1, late_corner)

    has_north, has_south = lat > 0, lat < n_lat - 1
    more_north, more_south = jnp.where(has_north, 1, 0), jnp.where(has_south, 1, 0)
    three = 1 + more_north + more_south
    width = x.shape[-1]
    half_tokens = LEVELS * SHIFT_H * 3 * TILE

    def device(dlon, dlat):
        return {"lon": lax.rem(lon + dlon + n_lon, n_lon), "lat": lax.rem(lat + dlat + n_lat, n_lat)}

    def exists(way):
        dlat = WAYS[way][1]
        return has_north if dlat < 0 else has_south if dlat > 0 else None

    def comes(way):
        dlat = WAYS[way][1]
        return has_south if dlat < 0 else has_north if dlat > 0 else None

    def when(condition, do):
        def run():
            do()

        if condition is None:
            run()
        else:
            pl.when(condition)(run)

    def signal_all(semaphore, ways):
        for way in ways:
            when(
                exists(way),
                lambda way=way: pl.semaphore_signal(
                    semaphore, inc=1, device_id=device(*WAYS[way]), device_id_type=MESH
                ),
            )

    def message(way, sources, send_index, target):
        dlon, dlat = WAYS[way]
        side = west if dlon > 0 else east
        if dlon == 0:
            landing = south if dlat < 0 else north
        else:
            landing = side.at[0] if dlat == 0 else side.at[1, :, pl.ds(3 if dlat < 0 else 0, 3)]
        return [
            pltpu.make_async_remote_copy(
                src_ref=source,
                dst_ref=place,
                send_sem=send_sem.at[send_index, part],
                recv_sem=recv_sem.at[way, part],
                device_id=device(*target),
                device_id_type=MESH,
            )
            for part, (source, place) in enumerate(zip(sources, (landing, halo_ids.at[way])))
        ]

    def direct(way):
        dlon, dlat = WAYS[way]
        rows = {0: pl.ds(0, 6), -1: pl.ds(0, 3), 1: pl.ds(3, 3)}[dlat]
        source = x_hbm.at[:, rows] if dlon == 0 else x_hbm.at[:, rows, 2 if dlon > 0 else 0]
        return message(way, (source, ids_hbm), way, WAYS[way])

    def send(ways):
        for way in ways:
            when(exists(way), lambda way=way: [copy.start() for copy in direct(way)])

    def wait_recv(ways):
        for way in ways:
            when(comes(way), lambda way=way: [copy.wait_recv() for copy in direct(way)])

    def wait_send(ways):
        for way in ways:
            when(exists(way), lambda way=way: [copy.wait_send() for copy in direct(way)])

    def chip_relays(way):
        source, edge = (north, has_north) if way == SOUTH else (south, has_south)
        to_east, to_west = (EAST_S, WEST_S) if way == SOUTH else (EAST_N, WEST_N)
        return [
            (
                jnp.logical_and(edge, even if dlon > 0 else odd),
                message(to, (source.at[:, :, 2 if dlon > 0 else 0], halo_ids.at[way]), to, (dlon, 0)),
            )
            for to, dlon in ((to_east, 1), (to_west, -1))
        ]

    def lat_relays(way):
        source = west if way == EAST else east
        parts = (
            (EAST_N if way == EAST else WEST_N, has_north, pl.ds(0, 3), -1),
            (EAST_S if way == EAST else WEST_S, has_south, pl.ds(3, 3), 1),
        )
        crossed = crossed_west if way == EAST else odd
        return [
            (
                jnp.logical_and(edge, crossed),
                message(to, (source.at[0, :, rows], halo_ids.at[way]), len(WAYS) + to, (0, dlat)),
            )
            for to, edge, rows, dlat in parts
        ]

    def start(relays):
        for condition, copies in relays:
            when(condition, lambda copies=copies: [copy.start() for copy in copies])

    def finish_relays(relays):
        for condition, copies in relays:
            when(condition, lambda copies=copies: [copy.wait_send() for copy in copies])

    barrier = pltpu.get_barrier_semaphore()
    ready_east, ready_west, ready_north, ready_south = [ready.at[index] for index in range(4)]
    to_east = jnp.logical_or(before, last)
    not_last = jnp.logical_not(last)
    early_east, early_west = east_first(lon), jnp.logical_not(east_first(lon - 1))
    late_east, late_west = jnp.logical_not(early_east), jnp.logical_not(early_west)
    inner_south = jnp.logical_and(has_south, not_last)
    inner_north = jnp.logical_and(has_north, not_last)
    early_south = jnp.logical_and(inner_south, south_first(lat))
    late_south = jnp.logical_and(inner_south, jnp.logical_not(south_first(lat)))
    early_north = jnp.logical_and(inner_north, jnp.logical_not(south_first(lat - 1)))
    late_north = jnp.logical_and(inner_north, south_first(lat - 1))
    seam = jnp.logical_or(first, last)

    pl.when(late_east)(lambda: signal_all(barrier, (EAST,)))
    pl.when(jnp.logical_and(late_west, jnp.logical_not(seam)))(lambda: signal_all(barrier, (WEST,)))
    pl.when(first)(lambda: signal_all(barrier, WESTWARD))
    pl.when(late_south)(lambda: signal_all(barrier, (SOUTH,)))
    pl.when(late_north)(lambda: signal_all(barrier, (NORTH,)))

    loads = [
        pltpu.make_async_copy(source, target, load_sem.at[index])
        for index, (source, target) in enumerate(
            ((x_hbm, x), (ids_hbm, ids), (w_qkv_hbm, w_qkv), (w_out_hbm, w_out))
        )
    ]

    def start_loads():
        for load in loads:
            load.start()

    pl.when(not_last)(start_loads)
    greeted = (
        jnp.where(early_west, 1, 0)
        + jnp.where(early_east, jnp.where(to_east, three, 1), 0)
        + jnp.where(jnp.logical_or(early_north, early_south), 1, 0)
        + jnp.where(jnp.logical_and(early_north, early_south), 1, 0)
    )

    @pl.when(greeted > 0)
    def _():
        pl.semaphore_wait(barrier, greeted)

    @pl.when(last)
    def _():
        signal_all(ready_west, (EAST,))
        send((EAST_N, EAST_S, EAST))
        signal_all(barrier, WESTWARD)
        start_loads()

    inner_east = jnp.logical_and(early_east, not_last)
    pl.when(early_north)(lambda: signal_all(ready_south, (NORTH,)))
    pl.when(early_south)(lambda: signal_all(ready_north, (SOUTH,)))
    pl.when(early_west)(lambda: signal_all(ready_east, (WEST,)))
    pl.when(inner_east)(lambda: signal_all(ready_west, (EAST,)))
    pl.when(early_west)(lambda: send((WEST,)))
    pl.when(early_south)(lambda: send((SOUTH,)))
    pl.when(early_north)(lambda: send((NORTH,)))
    pl.when(inner_east)(lambda: send((EAST,)))

    @pl.when(jnp.logical_not(has_north))
    def _():
        east[1, :, 0:3] = jnp.zeros((LEVELS, 3, TILE, width), BF16)
        west[1, :, 0:3] = jnp.zeros((LEVELS, 3, TILE, width), BF16)
        for way in (EAST_S, WEST_S):
            halo_ids[way] = jnp.zeros(halo_ids.shape[1:], jnp.int32)

    @pl.when(jnp.logical_not(has_south))
    def _():
        east[1, :, 3:6] = jnp.zeros((LEVELS, 3, TILE, width), BF16)
        west[1, :, 3:6] = jnp.zeros((LEVELS, 3, TILE, width), BF16)
        for way in (EAST_N, WEST_N):
            halo_ids[way] = jnp.zeros(halo_ids.shape[1:], jnp.int32)

    def class_of(ref, row, block):
        return ref[row, 0:1, block * SHIFT_W : block * SHIFT_W + 1]

    def classes(ref, row):
        return [class_of(ref, row, block) for block in range(4)]

    def query_code(half):
        return row_code(classes(ids, 3 * half), (half_tokens, 1), 0, 24)

    def project(source, first_feature):
        values = source.astype(F32).reshape(-1, width)
        center = jnp.mean(values, axis=-1, keepdims=True)
        spread = jnp.mean(jnp.square(values - center), axis=-1, keepdims=True)
        product = jnp.dot(
            values.astype(BF16), w_qkv[:, first_feature:], preferred_element_type=F32
        )
        return (product - center * w_sums[0:1, first_feature:]) * lax.rsqrt(spread + 1e-05)

    for load in loads[:3]:
        load.wait()
    block = (LEVELS, 3, 3, TILE, width)
    w_sums[...] = jnp.dot(
        jnp.ones((TILE, width), BF16), w_qkv[...], preferred_element_type=F32
    )
    for half in range(2):
        rows = slice(3 * half, 3 * half + 3)
        projected = project(x[:, rows], 0)
        queries[:, rows] = projected[:, :width].reshape(block)
        projected = projected.astype(BF16)
        key_code = row_code(classes(ids, 3 * half), (1, GROUP * half_tokens), 1, 24)
        ((some, total),) = attend(
            [
                (
                    projected[:, :width],
                    projected[:, width : 2 * width],
                    projected[:, 2 * width :],
                    bias_of(query_code(half), key_code),
                )
            ]
        )
        sums[:, rows] = some.reshape(block)
        totals[:, rows] = total.reshape(block)
        if half == 0:

            @pl.when(late_south)
            def _():
                pl.semaphore_wait(ready_south, 1)
                send((SOUTH,))

            @pl.when(last)
            def _():
                pl.semaphore_wait(ready_west, 1)
                send((NORTH, SOUTH, WEST))

    @pl.when(late_east)
    def _():
        pl.semaphore_wait(ready_east, 1)
        send((EAST,))

    @pl.when(late_north)
    def _():
        pl.semaphore_wait(ready_north, 1)
        send((NORTH,))

    @pl.when(jnp.logical_and(late_west, jnp.logical_not(seam)))
    def _():
        pl.semaphore_wait(ready_west, 1)
        send((WEST,))

    def row_halo(half):
        rows = pl.ds(3 * half, 3)
        both = project(beside[half], width).astype(BF16)
        key_vecs, values = both[:, :width], both[:, width:]
        their_ids = halo_ids.at[jnp.where(half == 0, SOUTH, NORTH)]
        key_code = row_code(classes(their_ids, 3 - 3 * half), (1, GROUP * half_tokens), 1, 24)
        ((some, total),) = attend(
            [
                (
                    queries[:, rows].reshape(half_tokens, width).astype(BF16),
                    key_vecs,
                    values,
                    bias_of(query_code(half), key_code),
                )
            ]
        )
        sums[:, rows] += some.reshape(block)
        totals[:, rows] += total.reshape(block)

    def side_halo(
        tile, source, part, ways, query_block, key_block, query_cols, key_cols, store=True
    ):
        straight, from_south, from_north = ways
        corner = part == 1
        tokens = LEVELS * 3 * TILE
        side = (LEVELS, 3, TILE, width)
        both = project(source[part], width).reshape(LEVELS, 6, TILE, 2 * width)
        query_col = lax.broadcasted_iota(jnp.int32, (tokens, 1), 0) % TILE
        key_col = lax.broadcasted_iota(jnp.int32, (1, GROUP * tokens), 1) % TILE
        sets = []
        for half, way, exists_there in ((0, from_north, more_north), (1, from_south, more_south)):
            rows = slice(3 * half, 3 * half + 3)
            there = halo_ids.at[jnp.where(corner, way, straight)]
            theirs = class_of(there, jnp.where(corner, 3 - 3 * half, 3 * half), key_block)
            theirs = jnp.where(jnp.logical_and(corner, exists_there == 0), -1, theirs)
            key_code = jnp.where((key_col >= key_cols[0]) & (key_col < key_cols[1]), theirs, -1)
            mine = class_of(ids, 3 * half, query_block)
            in_window = (query_col >= query_cols[0]) & (query_col < query_cols[1])
            vectors = both[:, rows].reshape(tokens, 2 * width).astype(BF16)
            sets.append(
                (
                    queries[:, rows, tile].reshape(tokens, width).astype(BF16),
                    vectors[:, :width],
                    vectors[:, width:],
                    bias_of(jnp.where(in_window, mine, -2), key_code),
                )
            )
        found = []
        for half, (some, total) in enumerate(attend(sets)):
            rows = slice(3 * half, 3 * half + 3)
            some = sums[:, rows, tile] + some.reshape(side)
            total = totals[:, rows, tile] + total.reshape(side)
            if not store:
                found.append((some / total).astype(BF16).reshape(tokens, width))
                continue
            sums[:, rows, tile] = some
            totals[:, rows, tile] = total
        return found

    def east_halo(part):
        side_halo(2, east, part, WESTWARD, 3, 0, (2, 8), (0, 6))

    def west_halo(part, store=True):
        return side_halo(0, west, part, EASTWARD, 0, 3, (0, 6), (2, 8), store)

    def finish(tiles):
        attended = (sums[:, :, tiles] / totals[:, :, tiles]).astype(BF16).reshape(-1, width)
        output = jnp.dot(attended, w_out[...], preferred_element_type=F32)
        patches = x[:, :, tiles].astype(F32)
        out_ref[:, :, tiles] = (patches + output.reshape(patches.shape)).astype(BF16)

    def relay_east():
        wait_recv((WEST,))
        start(lat_relays(WEST))

    def relay_west():
        wait_recv((EAST,))
        start(lat_relays(EAST))

    north_first = jnp.where(early_south | (last & south_first(lat)), 1, 0)
    for step in range(2):
        half = 1 - north_first if step == 0 else north_first
        if step == 0:
            pl.when(jnp.logical_and(odd, not_last))(relay_east)
            pl.when(jnp.logical_and(crossed_west, north_first == 1))(relay_west)

        @pl.when(half == 0)
        def _():
            wait_recv((SOUTH,))
            start(chip_relays(SOUTH))

        @pl.when(half == 1)
        def _():
            wait_recv((NORTH,))
            start(chip_relays(NORTH))

        @pl.when(jnp.where(half == 0, more_north, more_south) == 1)
        def _():
            row_halo(half)

        if step == 0:

            @pl.when(even)
            def _():
                wait_recv((WEST,))

            pl.when(not_last)(lambda: east_halo(0))
            pl.when(jnp.logical_and(crossed_west, north_first == 0))(relay_west)

            @pl.when(odd)
            def _():
                wait_recv((EAST,))

            @pl.when(jnp.logical_not(first))
            def _():
                west_halo(0)


            @pl.when(last)
            def _():
                relay_east()
                east_halo(0)

    @pl.when(first)
    def _():
        pl.semaphore_wait(ready_west, 1)
        send((WEST,))

    wait_recv((WEST_N, WEST_S))
    east_halo(1)
    loads[3].wait()
    finish(slice(1, 3))
    wait_send((EAST, WEST, NORTH, SOUTH))

    @pl.when(last)
    def _():
        wait_send((EAST_N, EAST_S))

    for way in (NORTH, SOUTH):
        finish_relays(chip_relays(way))
    for way in (EAST, WEST):
        finish_relays(lat_relays(way))

    straight_first = first & has_north & (lax.rem(lat, n_lat // 2) == 0)
    corners_first = jnp.logical_not(straight_first)

    @pl.when(straight_first)
    def _():
        wait_recv((EAST,))

    @pl.when(corners_first)
    def _():
        wait_recv((EAST_N, EAST_S))

    @pl.when(first)
    def _():
        west_halo(jnp.where(straight_first, 0, 1))


    @pl.when(straight_first)
    def _():
        wait_recv((EAST_N, EAST_S))

    @pl.when(jnp.logical_and(first, corners_first))
    def _():
        wait_recv((EAST,))

    attended = west_halo(jnp.where(jnp.logical_and(first, corners_first), 0, 1), store=False)
    output = jnp.dot(jnp.concatenate(attended, axis=0), w_out[...], preferred_element_type=F32)
    tokens = output.shape[0] // 2
    for half in range(2):
        rows = slice(3 * half, 3 * half + 3)
        patches = x[:, rows, 0].astype(F32)
        new = output[half * tokens : (half + 1) * tokens].reshape(patches.shape)
        out_ref[:, rows, 0] = (patches + new).astype(BF16)


def shards(n_lon, n_lat, patches, regions, w_qkv, w_out):
    levels, row_count, col_count, width = patches.shape
    tiles = (levels, row_count, col_count // TILE, TILE, width)
    half = (levels, SHIFT_H, col_count // TILE, TILE, width)
    side = (2, levels, row_count, TILE, width)
    id_shape = (row_count, levels, col_count)
    hbm = pl.BlockSpec(memory_space=pltpu.HBM)
    updated = pl.pallas_call(
        lambda *refs: kernel(n_lon, n_lat, *refs),
        out_shape=pltpu.VMEM(tiles, BF16),
        in_specs=[hbm] * 4,
        out_specs=pl.BlockSpec(memory_space=pltpu.VMEM),
        scratch_shapes=[
            pltpu.VMEM(tiles, BF16),
            pltpu.VMEM(w_qkv.shape, BF16),
            pltpu.VMEM(w_out.shape, BF16),
            pltpu.VMEM(id_shape, jnp.int32),
            pltpu.VMEM((2,) + half, BF16),
            pltpu.VMEM(side, BF16),
            pltpu.VMEM(side, BF16),
            pltpu.VMEM((len(WAYS),) + id_shape, jnp.int32),
            pltpu.VMEM((TILE, w_qkv.shape[1]), F32),
            pltpu.VMEM(tiles, F32),
            pltpu.VMEM(tiles, F32),
            pltpu.VMEM(tiles, F32),
            pltpu.SemaphoreType.DMA((4,)),
            pltpu.SemaphoreType.DMA((2 * len(WAYS), 2)),
            pltpu.SemaphoreType.DMA((len(WAYS), 2)),
            pltpu.SemaphoreType.REGULAR((4,)),
        ],
        compiler_params=pltpu.CompilerParams(
            collective_id=0, has_side_effects=True, vmem_limit_bytes=60 * 2**20
        ),
    )(patches.reshape(tiles), regions.transpose(1, 0, 2), w_qkv, w_out)
    return updated.reshape(patches.shape)


def solution(mesh):
    n_lon, n_lat = mesh.shape["lon"], mesh.shape["lat"]
    return jax.shard_map(
        lambda *arrays: shards(n_lon, n_lat, *arrays),
        mesh=mesh,
        in_specs=(P(None, "lat", "lon", None), P(None, "lat", "lon"), P(), P()),
        out_specs=P(None, "lat", "lon", None),
        check_vma=False,
    )
```
